256 devices in a mesh: tm: 64 (over x, y, z_lo), rows: 4 (over z_hi, core).
Axes of the slice: x: 4, y: 4, z: 8 (z_hi: 2, z_lo: 4; z = z_hi * 4 + z_lo), core: 2. Of those that a mesh axis runs over, the one named last changes fastest.
Arguments:
- band_blocks: bfloat16 [64, 3, 2048, 256], P('tm', None, 'rows'), may hold values from -0.21875 to 0.21875
- site_mask: int32 [64, 2048], P('tm', 'rows'), may hold values 0 or 1
- observed: float32 [64, 2048], P('tm', 'rows'), may hold values from -6 to 6
- band_offsets: int32 [64, 3], P('tm'), may hold values from -2 to 2, as said below
- site_gain: float32 [2048], P('rows'), may hold values from 0.2 to 0.9
Outputs:
- composed_matrix: bfloat16 [64, 2048, 2048], P('tm', 'rows')
- composed_offset: bfloat16 [64, 2048], P('tm', 'rows')
The draws below stay inside these ranges and needn't reach their ends.
Inputs may be any that keep to these rules, and one draw needn't show every extreme that they name: `band_offsets`: the 3 offsets of one step are distinct.
All inputs are finite; a program needn't handle non-finite values. No bound on the sum of `site_mask` on one device may be relied on, other than what follows from the above.
Results may differ from the reference program's by a relative error of at most 0.0062.
Values may be sent and summed in bfloat16 or wider, within the bound.
No kernel may reach another device: no remote copies, remote signals or barrier semaphores. Data moves between devices by JAX's collectives and lax.ppermute only.
A program may use at most 64 MiB of HBM per device.

```python
import math
import jax
import jax.numpy as jnp
from jax import lax

D = 2048
BLK = 256
NBAND = 3
NBLK = 8
TIMES = 64


def draw_band_offsets(key, part):
    key = jax.random.fold_in(key, 7)
    step_keys = jax.random.split(key, TIMES)

    def one_step(step_key):
        return jax.random.permutation(step_key, 5)[:NBAND] - 2
    return jax.vmap(one_step)(step_keys).astype(jnp.int32)


def touch_ends(array, rng, least, top_value):
    extent = array.shape
    index_at = [jax.random.randint(jax.random.fold_in(rng, axis), (), 0, extent[axis]) for axis in range(len(extent))]
    array = array.at[tuple(index_at)].set(least)
    longest = extent.index(max(extent))
    index_at[longest] = (index_at[longest] + 1) % extent[longest]
    return array.at[tuple(index_at)].set(top_value)


def level_of(own_key, dims, shards, low, top_value):
    def one(dim, blocks):
        draws = jax.random.uniform(jax.random.fold_in(jax.random.fold_in(own_key, 6), dim), (blocks,), jnp.float32, low / len(shards), top_value / len(shards))
        return jnp.repeat(jnp.exp(draws), dims[dim] // blocks).reshape((-1,) + (1,) * (len(dims) - dim - 1))

    gain = one(*shards[0])
    for cut in shards[1:]:
        gain = gain * one(*cut)
    return gain


def scatter_about(key, extent, scale, bound, cuts=(), held_as=jnp.bfloat16):
    gain = level_of(key, extent, cuts, -0.22, 0.18) if cuts else 1.0
    values = jax.random.normal(key, extent, jnp.float32) * scale * gain
    return jnp.minimum(jnp.maximum(values, -bound), bound).astype(held_as)


def setup_inputs(seed: int = 0) -> dict:
    splits = jax.random.split(jax.random.key(seed), 6)
    return {
        "band_blocks": scatter_about(splits[0], (TIMES, NBAND, D, BLK), (NBAND * BLK) ** -0.5, 0.21875, ((0, 64), (2, 4))),
        "site_mask": touch_ends((jax.random.randint(splits[1], (TIMES, D), 0, 2) < 1).astype(jnp.int32), jax.random.fold_in(splits[1], 1), 0, 1),
        "observed": scatter_about(splits[2], (TIMES, D), 1.0, 6.0, ((0, 64), (1, 4)), jnp.float32),
        "band_offsets": draw_band_offsets(jax.random.fold_in(splits[5], 71), 0),
        "site_gain": jnp.clip(jnp.exp(math.log(0.9) - 1.50407736 * jax.random.uniform(splits[4], (D,), jnp.float32) ** level_of(splits[4], (D,), ((0, 4),), -0.2, 0.2)), 0.2, 0.9),
    }


def placement_table(offsets):
    starts = jnp.arange(NBLK, dtype=jnp.int32)
    target = (starts[None, :] + offsets[:, None]) % NBLK
    columns = jnp.arange(NBLK, dtype=jnp.int32)
    return (columns[None, None, :] == target[:, :, None]).astype(jnp.float32)


def place_dense(scaled, table):
    blocks = scaled.astype(jnp.float32).reshape(NBAND, NBLK, BLK, BLK)
    dense = jnp.einsum('jrc,jrib->ricb', table, blocks)
    return dense.reshape(D, D).astype(jnp.bfloat16)


def doubling_level(matrices, offsets, distance):
    def combine_step(step):
        source = jnp.maximum(step - distance, 0)
        own_matrix = matrices[step]
        earlier = matrices[source]
        product = jnp.dot(own_matrix, earlier, preferred_element_type=jnp.float32)
        vector = jnp.dot(own_matrix, offsets[source], preferred_element_type=jnp.float32) + offsets[step].astype(jnp.float32)
        keep = step >= distance
        new_matrix = jnp.where(keep, product, own_matrix.astype(jnp.float32)).astype(jnp.bfloat16)
        new_vector = jnp.where(keep, vector, offsets[step].astype(jnp.float32)).astype(jnp.bfloat16)
        return new_matrix, new_vector
    return lax.map(combine_step, jnp.arange(TIMES, dtype=jnp.int32))


def reference(band_blocks, site_mask, observed, band_offsets, site_gain):
    factor = 1.0 - site_gain[None, :] * site_mask.astype(jnp.float32)
    scaled = (factor[:, None, :, None] * band_blocks.astype(jnp.float32)).astype(jnp.bfloat16)

    def build_step(step):
        return place_dense(scaled[step], placement_table(band_offsets[step]))

    level_matrix = lax.map(build_step, jnp.arange(TIMES, dtype=jnp.int32))
    level_offset = (site_gain[None, :] * site_mask.astype(jnp.float32) * observed).astype(jnp.bfloat16)
    level_matrix, level_offset = doubling_level(level_matrix, level_offset, 1)
    level_matrix, level_offset = doubling_level(level_matrix, level_offset, 2)
    return level_matrix, level_offset
```

```python
import functools

import jax
import jax.numpy as jnp
from jax import lax
from jax.experimental import pallas as pl
from jax.experimental.pallas import tpu as pltpu
from jax.sharding import PartitionSpec as P

BLK = 256
NBLK = 8
NBAND = 3
STEPS = 64
LOCAL = 512
BODY = NBAND * LOCAL
TOKEN = BODY + 16
CUTS = (0, 768, TOKEN)
AXES = ("tm", "rows")


def route(source, wanted=lambda step: True):
    pairs = []
    for step in range(STEPS):
        for half in range(2):
            if wanted(step):
                from_step, from_half = source(step, half)
                for core in range(2):
                    pairs.append(
                        ((from_step % STEPS) * 4 + from_half * 2 + core, step * 4 + half * 2 + core)
                    )
    return pairs


UP = route(lambda t, h: (t - 1, h if t % 4 > 0 else 1 - h))
DOWN = route(lambda t, h: (t + 1, h if t % 4 < 3 else 1 - h))
ACROSS = route(lambda t, h: (t - 4, h) if t % 4 > 0 else (t, h))
LEVEL_DOWN = route(lambda t, h: (t + 1, h) if t % 4 < 3 else (t - 3, 1 - h))
SIBLING = [(i, i ^ 1) for i in range(STEPS * 4)]


def prepare_kernel(offsets_ref, band_ref, mask_ref, observed_ref, gain_ref, *outs):
    flag = mask_ref[...].astype(jnp.float32)
    gain = gain_ref[...]
    factor = 1.0 - gain * flag
    vector = gain * flag * observed_ref[...]
    for i in range(LOCAL // 128):
        column = jnp.transpose(
            jnp.broadcast_to(factor[:, i * 128 : (i + 1) * 128], (128, 128))
        )
        for j in range(NBAND):
            top = j * LOCAL + i * 128
            piece = max(n for n in range(len(outs)) if CUTS[n] <= top)
            at = top - CUTS[piece]
            for side in range(2):
                lanes = slice(side * 128, side * 128 + 128)
                block = band_ref[0, j, i * 128 : (i + 1) * 128, lanes].astype(jnp.float32)
                outs[piece][at : at + 128, lanes] = (column * block).astype(jnp.bfloat16)
    row = lax.broadcasted_iota(jnp.int32, (16, BLK), 0)
    lane = lax.broadcasted_iota(jnp.int32, (16, BLK), 1)
    tile = jnp.where(row == 0, jnp.broadcast_to(vector[:, :BLK], (16, BLK)), 0.0)
    tile = jnp.where(row == 1, jnp.broadcast_to(vector[:, BLK:], (16, BLK)), tile)
    for j in range(NBAND):
        shift = offsets_ref[0, j].astype(jnp.float32)
        tile = jnp.where((row == 2) & (lane == j), shift, tile)
    at = BODY - CUTS[-2]
    outs[-1][at : at + 16, :] = tile.astype(jnp.bfloat16)


def prepare(band, mask, observed, offsets, gain):
    vmem = pl.BlockSpec(memory_space=pltpu.VMEM)
    return pl.pallas_call(
        prepare_kernel,
        out_shape=[
            jax.ShapeDtypeStruct((b - a, BLK), jnp.bfloat16) for a, b in zip(CUTS, CUTS[1:])
        ],
        in_specs=[pl.BlockSpec(memory_space=pltpu.SMEM)] + [vmem] * 4,
        out_specs=[vmem] * (len(CUTS) - 1),
    )(offsets, band, mask, observed, gain.reshape(1, LOCAL))


def tile_of(ref):
    return ref[BODY : BODY + 16, :].astype(jnp.float32)


def shifts_of(tile):
    row = lax.broadcasted_iota(jnp.int32, (16, BLK), 0)
    lane = lax.broadcasted_iota(jnp.int32, (16, BLK), 1)
    return [
        jnp.sum(jnp.where((row == 2) & (lane == j), tile, 0.0)).astype(jnp.int32)
        for j in range(NBAND)
    ]


def compose_kernel(*refs):
    pieces = len(CUTS) - 1
    arrived = refs[: 13 * pieces]
    matrix_ref, vector_ref = refs[13 * pieces : 13 * pieces + 2]
    own, earlier, factor_a, factor_b, total, own_sem, sems, out_sems = refs[13 * pieces + 2 :]
    step = lax.axis_index("tm")
    place = lax.axis_index("rows")
    half, core = place // 2, place % 2
    phase = step % 4

    own_copies = [
        pltpu.make_async_copy(arrived[n], own.at[CUTS[n] : CUTS[n + 1]], own_sem.at[n])
        for n in range(pieces)
    ]
    copies = [[], [], []]
    for level in range(3):
        side = jnp.where(phase >= level + 1, half, 1 - half)
        groups = [2 * side + core, 2 * side + 1 - core]
        groups += [2 * (1 - side) + core, 2 * (1 - side) + 1 - core]
        for source in range(4):
            for n in range(pieces):
                copies[level].append(
                    pltpu.make_async_copy(
                        arrived[(1 + level * 4 + source) * pieces + n],
                        earlier.at[level, groups[source], CUTS[n] : CUTS[n + 1]],
                        sems.at[level, source, n],
                    )
                )
    for copy in own_copies + copies[0] + copies[1] + copies[2]:
        copy.start()

    factor_a[...] = jnp.zeros_like(factor_a)
    total[...] = jnp.zeros_like(total)
    for copy in own_copies:
        copy.wait()
    own_tile = tile_of(own)
    own_shifts = shifts_of(own_tile)
    for j in range(NBAND):
        for r in range(2):
            target = lax.rem(2 * place + r + own_shifts[j] + NBLK, NBLK)
            factor_a[target, r * BLK : (r + 1) * BLK, :] = own[
                (2 * j + r) * BLK : (2 * j + r + 1) * BLK, :
            ]

    row = lax.broadcasted_iota(jnp.int32, (16, BLK), 0)
    buffers = [factor_a, factor_b]
    for level in range(3):
        source, target = buffers[level % 2], buffers[(level + 1) % 2]
        for copy in copies[level]:
            copy.wait()

        @pl.when(step > level)
        def _():
            shifts = shifts_of(tile_of(earlier.at[level, 0]))

            @pl.loop(0, NBLK)
            def _(c):
                product = None
                for j in range(NBAND):
                    k = lax.rem(c - shifts[j] + NBLK, NBLK)
                    at = pl.multiple_of((2 * j + k % 2) * BLK, BLK)
                    term = jnp.dot(
                        source[k],
                        earlier[level, k // 2, pl.ds(at, BLK), :],
                        preferred_element_type=jnp.float32,
                    )
                    product = term if product is None else product + term
                target[c] = product.astype(jnp.bfloat16)
                tile = tile_of(earlier.at[level, c // 2])
                vector = jnp.sum(jnp.where(row == c % 2, tile, 0.0), axis=0, keepdims=True)
                total[...] += source[c].astype(jnp.float32) * vector

        @pl.when(step <= level)
        def _():
            target[...] = source[...]

    result = buffers[1]
    writes = [
        pltpu.make_async_copy(
            result.at[c], matrix_ref.at[0, :, c * BLK : (c + 1) * BLK], out_sems.at[c]
        )
        for c in range(NBLK)
    ]
    for write in writes:
        write.start()
    value = total[...]
    high = value.astype(jnp.bfloat16)
    low = (value - high.astype(jnp.float32)).astype(jnp.bfloat16)
    ones = jnp.ones((16, BLK), jnp.bfloat16)
    sums = sum(
        lax.dot_general(
            ones, part, (((1,), (1,)), ((), ())), preferred_element_type=jnp.float32
        )
        for part in (high, low)
    )
    for r in range(2):
        vector_ref[:, r * BLK : (r + 1) * BLK] = (
            sums[0:1, r * BLK : (r + 1) * BLK] + own_tile[r : r + 1, :]
        ).astype(jnp.bfloat16)
    for write in writes:
        write.wait()


def compose(arrived):
    pieces = len(CUTS) - 1
    anywhere = pl.BlockSpec(memory_space=pl.ANY)
    return pl.pallas_call(
        compose_kernel,
        out_shape=[
            jax.ShapeDtypeStruct((1, LOCAL, NBLK * BLK), jnp.bfloat16),
            jax.ShapeDtypeStruct((1, LOCAL), jnp.bfloat16),
        ],
        in_specs=[anywhere] * len(arrived),
        out_specs=[anywhere, pl.BlockSpec(memory_space=pltpu.VMEM)],
        scratch_shapes=[
            pltpu.VMEM((TOKEN, BLK), jnp.bfloat16),
            pltpu.VMEM((3, 4, TOKEN, BLK), jnp.bfloat16),
            pltpu.VMEM((NBLK, LOCAL, BLK), jnp.bfloat16),
            pltpu.VMEM((NBLK, LOCAL, BLK), jnp.bfloat16),
            pltpu.VMEM((LOCAL, BLK), jnp.float32),
            pltpu.SemaphoreType.DMA((pieces,)),
            pltpu.SemaphoreType.DMA((3, 4, pieces)),
            pltpu.SemaphoreType.DMA((NBLK,)),
        ],
        compiler_params=pltpu.CompilerParams(vmem_limit_bytes=28 * 1024 * 1024),
    )(*arrived)


def per_device(band_blocks, site_mask, observed, band_offsets, site_gain):
    move = functools.partial(lax.ppermute, axis_name=AXES)
    own = prepare(band_blocks, site_mask, observed, band_offsets, site_gain)
    ups, downs = [], []
    for piece in own:
        across = move(piece, perm=ACROSS)
        up = [move(piece, perm=UP)]
        down = [move(across, perm=LEVEL_DOWN)]
        for _ in range(2):
            up.append(move(up[-1], perm=UP))
            down.append(move(down[-1], perm=DOWN))
        ups.append(up)
        downs.append(down)
    arrived = list(own)
    for level in range(3):
        for chain in ([up[level] for up in ups], [down[2 - level] for down in downs]):
            arrived += chain
            arrived += [move(piece, perm=SIBLING) for piece in chain]
    return tuple(compose(arrived))


def solution(mesh):
    in_specs = (
        P("tm", None, "rows", None),
        P("tm", "rows"),
        P("tm", "rows"),
        P("tm", None),
        P("rows"),
    )
    out_specs = (P("tm", "rows", None), P("tm", "rows"))
    return jax.shard_map(
        per_device, mesh=mesh, in_specs=in_specs, out_specs=out_specs, check_vma=False
    )
```

```python
import functools

import jax
import jax.numpy as jnp
from jax import lax
from jax.experimental import pallas as pl
from jax.experimental.pallas import tpu as pltpu
from jax.sharding import PartitionSpec as P

BLK = 256
NBLK = 8
NBAND = 3
STEPS = 64
LOCAL = 512
TILE = 16
TOKEN = TILE + NBAND * LOCAL
CUT = TILE + 384
AXES = ("tm", "rows")


def route(source):
    pairs = []
    for step in range(STEPS):
        for half in range(2):
            from_step, from_half = source(step, half)
            for core in range(2):
                pairs.append(
                    ((from_step % STEPS) * 4 + from_half * 2 + core, step * 4 + half * 2 + core)
                )
    return pairs


UP = route(lambda t, h: (t - 1, h if t % 4 > 0 else 1 - h))
DOWN = route(lambda t, h: (t + 1, h if t % 4 < 3 else 1 - h))
FIRST_DOWN = route(lambda t, h: (t - 3, h if t % 4 < 3 else 1 - h))
ACROSS = route(lambda t, h: (t - 4, h) if t % 4 == 3 else (t, h))
LEVEL_UP = route(lambda t, h: (t - 1, h) if t % 4 > 0 else (t + 3, 1 - h))
SIBLING = [(i, i ^ 1) for i in range(STEPS * 4)]


def store(outs, top, value, lanes=slice(0, BLK)):
    rows = value.shape[0]
    whole, low, high = outs
    whole[top : top + rows, lanes] = value
    if top + rows <= CUT:
        low[top : top + rows, lanes] = value
    else:
        high[top - CUT : top - CUT + rows, lanes] = value


def prepare_kernel(offsets_ref, band_ref, mask_ref, observed_ref, gain_ref, *outs):
    flag = mask_ref[...].astype(jnp.float32)
    gain = gain_ref[...]
    factor = 1.0 - gain * flag
    vector = gain * flag * observed_ref[...]
    row = lax.broadcasted_iota(jnp.int32, (TILE, BLK), 0)
    lane = lax.broadcasted_iota(jnp.int32, (TILE, BLK), 1)
    tile = jnp.where(row == 0, jnp.broadcast_to(vector[:, :BLK], (TILE, BLK)), 0.0)
    tile = jnp.where(row == 1, jnp.broadcast_to(vector[:, BLK:], (TILE, BLK)), tile)
    for j in range(NBAND):
        shift = offsets_ref[0, j].astype(jnp.float32)
        tile = jnp.where((row == 2) & (lane == j), shift, tile)
    store(outs, 0, tile.astype(jnp.bfloat16))
    for i in range(LOCAL // 128):
        column = jnp.transpose(
            jnp.broadcast_to(factor[:, i * 128 : (i + 1) * 128], (128, 128))
        )
        for j in range(NBAND):
            for side in range(2):
                lanes = slice(side * 128, side * 128 + 128)
                block = band_ref[0, j, i * 128 : (i + 1) * 128, lanes].astype(jnp.float32)
                top = TILE + j * LOCAL + i * 128
                store(outs, top, (column * block).astype(jnp.bfloat16), lanes)


def prepare(band, mask, observed, offsets, gain):
    vmem = pl.BlockSpec(memory_space=pltpu.VMEM)
    return pl.pallas_call(
        prepare_kernel,
        out_shape=[
            jax.ShapeDtypeStruct((rows, BLK), jnp.bfloat16) for rows in (TOKEN, CUT, TOKEN - CUT)
        ],
        in_specs=[pl.BlockSpec(memory_space=pltpu.SMEM)] + [vmem] * 4,
        out_specs=[vmem] * 3,
    )(offsets, band, mask, observed, gain.reshape(1, LOCAL))


def tile_of(ref):
    return ref[:TILE, :].astype(jnp.float32)


def shifts_of(tile):
    row = lax.broadcasted_iota(jnp.int32, (TILE, BLK), 0)
    lane = lax.broadcasted_iota(jnp.int32, (TILE, BLK), 1)
    return [
        jnp.sum(jnp.where((row == 2) & (lane == j), tile, 0.0)).astype(jnp.int32)
        for j in range(NBAND)
    ]


def place_of(step, place, distance):
    half, core = place // 2, place % 2
    side = jnp.where(step % 4 >= distance, half, 1 - half)
    return [
        2 * side + core,
        2 * side + 1 - core,
        2 * (1 - side) + core,
        2 * (1 - side) + 1 - core,
    ]


def gather(refs, whole, groups, sems):
    low, high, sibling_low, sibling_high, down, sibling_down = refs
    parts = [
        (low, groups[0], 0, CUT),
        (high, groups[0], CUT, TOKEN),
        (sibling_low, groups[1], 0, CUT),
        (sibling_high, groups[1], CUT, TOKEN),
        (down, groups[2], 0, TOKEN),
        (sibling_down, groups[3], 0, TOKEN),
    ]
    return [
        pltpu.make_async_copy(ref, whole.at[group, a:b], sems.at[n])
        for n, (ref, group, a, b) in enumerate(parts)
    ]


def column_of(source, earlier, shifts, c):
    product = None
    for j in range(NBAND):
        k = lax.rem(c - shifts[j] + NBLK, NBLK)
        at = pl.multiple_of(TILE + (2 * j + k % 2) * BLK, TILE)
        term = jnp.dot(
            source[k], earlier[k // 2, pl.ds(at, BLK), :], preferred_element_type=jnp.float32
        )
        product = term if product is None else product + term
    return product


def vector_of(tiles, c):
    return tiles[c // 2][c % 2 : c % 2 + 1, :]


def pair_kernel(*refs):
    own, first, second, last = refs[0], refs[1:7], refs[7:13], refs[13:17]
    product_ref, vector_ref = refs[17:19]
    near, far, bare, level, total, tiles, near_sems, far_sems, tile_sems = refs[19:]
    step, place = lax.axis_index("tm"), lax.axis_index("rows")

    near_copies = gather(first, near, place_of(step, place, 1), near_sems)
    far_copies = gather(second, far, place_of(step, place, 2), far_sems)
    groups = place_of(step, place, 3)
    tile_copies = [
        pltpu.make_async_copy(ref.at[0:TILE], tiles.at[group], tile_sems.at[n])
        for n, (ref, group) in enumerate(zip(last, groups))
    ]
    for copy in near_copies + tile_copies + far_copies:
        copy.start()

    bare[...] = jnp.zeros_like(bare)
    own_tile = tile_of(own)
    own_shifts = shifts_of(own_tile)
    for j in range(NBAND):
        for r in range(2):
            target = lax.rem(2 * place + r + own_shifts[j] + NBLK, NBLK)
            at = TILE + (2 * j + r) * BLK
            bare[target, r * BLK : (r + 1) * BLK, :] = own[at : at + BLK, :]
    for copy in near_copies + tile_copies:
        copy.wait()

    near_tiles = [tile_of(near.at[g]) for g in range(4)]
    total[...] = jnp.zeros_like(total)

    @pl.when(step >= 1)
    def _():
        shifts = shifts_of(near_tiles[0])
        for c in range(NBLK):
            level[c] = column_of(bare, near, shifts, c).astype(jnp.bfloat16)
            total[...] += bare[c].astype(jnp.float32) * vector_of(near_tiles, c)

    @pl.when(step < 1)
    def _():
        level[...] = bare[...]

    for copy in far_copies:
        copy.wait()
    far_tiles = [tile_of(far.at[g]) for g in range(4)]

    @pl.when(step >= 2)
    def _():
        shifts = shifts_of(far_tiles[0])
        for c in range(NBLK):
            product_ref[c] = column_of(level, far, shifts, c).astype(jnp.bfloat16)
            total[...] += level[c].astype(jnp.float32) * vector_of(far_tiles, c)

    @pl.when(step < 2)
    def _():
        product_ref[...] = level[...]

    @pl.when(step >= 3)
    def _():
        last_tiles = [tile_of(tiles.at[g]) for g in range(4)]
        value = total[...]
        for c in range(NBLK):
            value = value + product_ref[c].astype(jnp.float32) * vector_of(last_tiles, c)
        total[...] = value

    value = total[...]
    high = value.astype(jnp.bfloat16)
    low = (value - high.astype(jnp.float32)).astype(jnp.bfloat16)
    ones = jnp.ones((TILE, BLK), jnp.bfloat16)
    sums = sum(
        lax.dot_general(ones, part, (((1,), (1,)), ((), ())), preferred_element_type=jnp.float32)
        for part in (high, low)
    )
    for r in range(2):
        vector_ref[:, r * BLK : (r + 1) * BLK] = (
            sums[0:1, r * BLK : (r + 1) * BLK] + own_tile[r : r + 1, :]
        ).astype(jnp.bfloat16)


def pair(own, first, second, last):
    anywhere, vmem = pl.BlockSpec(memory_space=pl.ANY), pl.BlockSpec(memory_space=pltpu.VMEM)
    arrived = [own, *first, *second, *last]
    return pl.pallas_call(
        pair_kernel,
        out_shape=[
            jax.ShapeDtypeStruct((NBLK, LOCAL, BLK), jnp.bfloat16),
            jax.ShapeDtypeStruct((1, LOCAL), jnp.bfloat16),
        ],
        in_specs=[vmem] + [anywhere] * (len(arrived) - 1),
        out_specs=[vmem, vmem],
        scratch_shapes=[
            pltpu.VMEM((4, TOKEN, BLK), jnp.bfloat16),
            pltpu.VMEM((4, TOKEN, BLK), jnp.bfloat16),
            pltpu.VMEM((NBLK, LOCAL, BLK), jnp.bfloat16),
            pltpu.VMEM((NBLK, LOCAL, BLK), jnp.bfloat16),
            pltpu.VMEM((LOCAL, BLK), jnp.float32),
            pltpu.VMEM((4, TILE, BLK), jnp.bfloat16),
            pltpu.SemaphoreType.DMA((6,)),
            pltpu.SemaphoreType.DMA((6,)),
            pltpu.SemaphoreType.DMA((4,)),
        ],
        compiler_params=pltpu.CompilerParams(vmem_limit_bytes=24 * 1024 * 1024),
        cost_estimate=pl.CostEstimate(
            flops=96 * 2 * BLK**3, bytes_accessed=10 * 2**20, transcendentals=0
        ),
    )(*arrived)


def last_kernel(*refs):
    before_ref, third, matrix_ref = refs[0], refs[1:7], refs[7]
    before, earlier, result, before_sem, sems, out_sems = refs[8:]
    step, place = lax.axis_index("tm"), lax.axis_index("rows")
    before_copy = pltpu.make_async_copy(before_ref, before, before_sem.at[0])
    copies = gather(third, earlier, place_of(step, place, 3), sems)
    for copy in [before_copy] + copies:
        copy.start()
    for copy in [before_copy] + copies:
        copy.wait()
    writes = [
        pltpu.make_async_copy(
            result.at[c], matrix_ref.at[0, :, c * BLK : (c + 1) * BLK], out_sems.at[c]
        )
        for c in range(NBLK)
    ]

    @pl.when(step >= 3)
    def _():
        shifts = shifts_of(tile_of(earlier.at[0]))
        for c in range(NBLK):
            result[c] = column_of(before, earlier, shifts, c).astype(jnp.bfloat16)
            writes[c].start()

    @pl.when(step < 3)
    def _():
        for c in range(NBLK):
            result[c] = before[c]
            writes[c].start()

    for write in writes:
        write.wait()


def last(before, third):
    anywhere = pl.BlockSpec(memory_space=pl.ANY)
    return pl.pallas_call(
        last_kernel,
        out_shape=jax.ShapeDtypeStruct((1, LOCAL, NBLK * BLK), jnp.bfloat16),
        in_specs=[anywhere] * 7,
        out_specs=anywhere,
        scratch_shapes=[
            pltpu.VMEM((NBLK, LOCAL, BLK), jnp.bfloat16),
            pltpu.VMEM((4, TOKEN, BLK), jnp.bfloat16),
            pltpu.VMEM((NBLK, LOCAL, BLK), jnp.bfloat16),
            pltpu.SemaphoreType.DMA((1,)),
            pltpu.SemaphoreType.DMA((6,)),
            pltpu.SemaphoreType.DMA((NBLK,)),
        ],
        compiler_params=pltpu.CompilerParams(vmem_limit_bytes=24 * 1024 * 1024),
        cost_estimate=pl.CostEstimate(
            flops=48 * 2 * BLK**3, bytes_accessed=7 * 2**20, transcendentals=0
        ),
    )(before, *third)


def after(values, *done):
    return list(lax.optimization_barrier((tuple(values), done))[0])


def per_device(band_blocks, site_mask, observed, band_offsets, site_gain):
    move = functools.partial(lax.ppermute, axis_name=AXES)
    swap = functools.partial(move, perm=SIBLING)
    own, low, high = prepare(band_blocks, site_mask, observed, band_offsets, site_gain)
    down1 = move(own, perm=FIRST_DOWN)
    low0, high0 = move(low, perm=ACROSS), move(high, perm=ACROSS)
    low1 = move(low0, perm=LEVEL_UP)
    low2 = move(low1, perm=UP)
    low3 = move(low2, perm=UP)
    (high0,) = after([high0], low3)
    high1 = move(high0, perm=LEVEL_UP)
    down1, low1, low2 = after([down1, low1, low2], high0)
    down2 = move(down1, perm=DOWN)
    down1, low1, low2, low3 = after([down1, low1, low2, low3], high1)
    swaps1 = [swap(x) for x in (down1, low1, low2, low3)]
    high2 = move(high1, perm=UP)
    (down2,) = after([down2], high1)
    down3 = move(down2, perm=DOWN)
    high1, down2 = after([high1, down2], down2)
    swaps2 = [swap(x) for x in (high1, down2)]
    high3 = move(high2, perm=UP)
    swaps3 = [swap(x) for x in (high2, down3)]
    low3, swaps1[3], down1, swaps1[0] = after([low3, swaps1[3], down1, swaps1[0]], high3)
    product, vector = pair(
        own,
        (low1, high1, swaps1[1], swaps2[0], down3, swaps3[1]),
        (low2, high2, swaps1[2], swaps3[0], down2, swaps2[1]),
        (low3, swaps1[3], down1, swaps1[0]),
    )
    matrix = last(product, (low3, high3, swaps1[3], swap(high3), down1, swaps1[0]))
    return matrix, vector


def solution(mesh):
    in_specs = (
        P("tm", None, "rows", None),
        P("tm", "rows"),
        P("tm", "rows"),
        P("tm", None),
        P("rows"),
    )
    out_specs = (P("tm", "rows", None), P("tm", "rows"))
    return jax.shard_map(
        per_device, mesh=mesh, in_specs=in_specs, out_specs=out_specs, check_vma=False
    )
```

```python
import functools

import jax
import jax.numpy as jnp
from jax import lax
from jax.experimental import pallas as pl
from jax.experimental.pallas import tpu as pltpu
from jax.sharding import PartitionSpec as P

BLK = 256
NBLK = 8
NBAND = 3
STEPS = 64
LOCAL = 512
TILE = 16
TOKEN = TILE + NBAND * LOCAL
AXES = ("tm", "rows")


def route(up, down):
    pairs = []
    for step in range(STEPS):
        for half in range(2):
            for core, source in enumerate((up, down)):
                from_step, from_half = source(step, half)
                pairs.append(
                    ((from_step % STEPS) * 4 + from_half * 2 + core, step * 4 + half * 2 + core)
                )
    return pairs


def above(t, h):
    return t + 1, h if t % 4 < 3 else 1 - h


def below(t, h):
    return t - 1, h if t % 4 > 0 else 1 - h


HOPS = (
    route(
        lambda t, h: (t - 4, h) if t % 4 == 3 else (t, h),
        lambda t, h: (t - 3, h if t % 4 < 3 else 1 - h),
    ),
    route(lambda t, h: (t - 1, h) if t % 4 > 0 else (t + 3, 1 - h), above),
    route(below, above),
    route(below, lambda t, h: (t, h)),
)
SIBLING = [(i, i ^ 1) for i in range(STEPS * 4)]


def prepare_kernel(offsets_ref, band_ref, mask_ref, observed_ref, gain_ref, token_ref):
    flag = mask_ref[...].astype(jnp.float32)
    gain = gain_ref[...]
    factor = 1.0 - gain * flag
    vector = gain * flag * observed_ref[...]
    row = lax.broadcasted_iota(jnp.int32, (TILE, BLK), 0)
    lane = lax.broadcasted_iota(jnp.int32, (TILE, BLK), 1)
    tile = jnp.where(row == 0, jnp.broadcast_to(vector[:, :BLK], (TILE, BLK)), 0.0)
    tile = jnp.where(row == 1, jnp.broadcast_to(vector[:, BLK:], (TILE, BLK)), tile)
    for j in range(NBAND):
        shift = offsets_ref[0, j].astype(jnp.float32)
        tile = jnp.where((row == 2) & (lane == j), shift, tile)
    token_ref[:TILE, :] = tile.astype(jnp.bfloat16)
    for i in range(LOCAL // 128):
        column = jnp.transpose(
            jnp.broadcast_to(factor[:, i * 128 : (i + 1) * 128], (128, 128))
        )
        for j in range(NBAND):
            for side in range(2):
                lanes = slice(side * 128, side * 128 + 128)
                block = band_ref[0, j, i * 128 : (i + 1) * 128, lanes].astype(jnp.float32)
                top = TILE + j * LOCAL + i * 128
                token_ref[top : top + 128, lanes] = (column * block).astype(jnp.bfloat16)


def prepare(band, mask, observed, offsets, gain):
    vmem = pl.BlockSpec(memory_space=pltpu.VMEM)
    return pl.pallas_call(
        prepare_kernel,
        out_shape=jax.ShapeDtypeStruct((TOKEN, BLK), jnp.bfloat16),
        in_specs=[pl.BlockSpec(memory_space=pltpu.SMEM)] + [vmem] * 4,
        out_specs=vmem,
    )(offsets, band, mask, observed, gain.reshape(1, LOCAL))


def tile_of(ref):
    return ref[:TILE, :].astype(jnp.float32)


def shifts_of(tile):
    row = lax.broadcasted_iota(jnp.int32, (TILE, BLK), 0)
    lane = lax.broadcasted_iota(jnp.int32, (TILE, BLK), 1)
    return [
        jnp.sum(jnp.where((row == 2) & (lane == j), tile, 0.0)).astype(jnp.int32)
        for j in range(NBAND)
    ]


def gather(refs, whole, distance, sems):
    step, place = lax.axis_index("tm"), lax.axis_index("rows")
    half = place // 2
    side = jnp.where(step % 4 >= distance, half, 1 - half)
    groups = [2 * side, 2 * side + 1, 2 * (1 - side) + 1, 2 * (1 - side)]
    rows = whole.shape[1]
    pairs = [
        [
            pltpu.make_async_copy(refs[4 * core + n].at[0:rows], whole.at[groups[n]], sems.at[n])
            for n in range(4)
        ]
        for core in range(2)
    ]

    def start():
        for core in range(2):

            @pl.when(place % 2 == core)
            def _():
                for copy in pairs[core]:
                    copy.start()

    def wait():
        for copy in pairs[0]:
            copy.wait()

    return start, wait


def column_of(source, earlier, shifts, c):
    product = None
    for j in range(NBAND):
        k = lax.rem(c - shifts[j] + NBLK, NBLK)
        at = pl.multiple_of(TILE + (2 * j + k % 2) * BLK, TILE)
        term = jnp.dot(
            source[k], earlier[k // 2, pl.ds(at, BLK), :], preferred_element_type=jnp.float32
        )
        product = term if product is None else product + term
    return product


def vector_of(tiles, c):
    return tiles[c // 2][c % 2 : c % 2 + 1, :]


def place_kernel(own_ref, bare_ref, vector_ref):
    place = lax.axis_index("rows")
    tile = tile_of(own_ref)
    shifts = shifts_of(tile)
    bare_ref[...] = jnp.zeros_like(bare_ref)
    for j in range(NBAND):
        for r in range(2):
            target = lax.rem(2 * place + r + shifts[j] + NBLK, NBLK)
            at = TILE + (2 * j + r) * BLK
            bare_ref[target, r * BLK : (r + 1) * BLK, :] = own_ref[at : at + BLK, :]
    for r in range(2):
        vector_ref[:, r * BLK : (r + 1) * BLK] = tile[r : r + 1, :]


def place_blocks(own):
    vmem = pl.BlockSpec(memory_space=pltpu.VMEM)
    return pl.pallas_call(
        place_kernel,
        out_shape=[
            jax.ShapeDtypeStruct((NBLK, LOCAL, BLK), jnp.bfloat16),
            jax.ShapeDtypeStruct((1, LOCAL), jnp.float32),
        ],
        in_specs=[vmem],
        out_specs=[vmem, vmem],
        cost_estimate=pl.CostEstimate(flops=0, bytes_accessed=3 * 2**20, transcendentals=0),
    )(own)


def pair_kernel(*refs):
    bare_ref, first, second = refs[0], refs[1:9], refs[9:17]
    product_ref, total = refs[17:19]
    near, far, bare, level, bare_sem, near_sems, far_sems = refs[19:]
    step, place = lax.axis_index("tm"), lax.axis_index("rows")
    near_start, near_wait = gather(first, near, 1, near_sems)
    far_start, far_wait = gather(second, far, 2, far_sems)
    bare_copy = pltpu.make_async_copy(bare_ref, bare, bare_sem.at[0])
    bare_copy.start()
    near_start()
    far_start()

    total[...] = jnp.zeros_like(total)
    bare_copy.wait()
    near_wait()

    @pl.when(step >= 1)
    def _():
        tiles = [tile_of(near.at[g]) for g in range(4)]
        shifts = shifts_of(tiles[0])
        for c in range(NBLK):
            level[c] = column_of(bare, near, shifts, c).astype(jnp.bfloat16)
            total[...] += bare[c].astype(jnp.float32) * vector_of(tiles, c)

    @pl.when(step < 1)
    def _():
        level[...] = bare[...]

    far_wait()

    @pl.when(step >= 2)
    def _():
        tiles = [tile_of(far.at[g]) for g in range(4)]
        shifts = shifts_of(tiles[0])
        for c in range(NBLK):
            product_ref[c] = column_of(level, far, shifts, c).astype(jnp.bfloat16)
            total[...] += level[c].astype(jnp.float32) * vector_of(tiles, c)

    @pl.when(step < 2)
    def _():
        product_ref[...] = level[...]


def pair(bare, first, second):
    anywhere, vmem = pl.BlockSpec(memory_space=pl.ANY), pl.BlockSpec(memory_space=pltpu.VMEM)
    return pl.pallas_call(
        pair_kernel,
        out_shape=[
            jax.ShapeDtypeStruct((NBLK, LOCAL, BLK), jnp.bfloat16),
            jax.ShapeDtypeStruct((LOCAL, BLK), jnp.float32),
        ],
        in_specs=[anywhere] * 17,
        out_specs=[vmem, vmem],
        scratch_shapes=[
            pltpu.VMEM((4, TOKEN, BLK), jnp.bfloat16),
            pltpu.VMEM((4, TOKEN, BLK), jnp.bfloat16),
            pltpu.VMEM((NBLK, LOCAL, BLK), jnp.bfloat16),
            pltpu.VMEM((NBLK, LOCAL, BLK), jnp.bfloat16),
            pltpu.SemaphoreType.DMA((1,)),
            pltpu.SemaphoreType.DMA((4,)),
            pltpu.SemaphoreType.DMA((4,)),
        ],
        compiler_params=pltpu.CompilerParams(vmem_limit_bytes=24 * 1024 * 1024),
        cost_estimate=pl.CostEstimate(
            flops=96 * 2 * BLK**3, bytes_accessed=10 * 2**20, transcendentals=0
        ),
    )(bare, *first, *second)


def last_kernel(*refs):
    before_ref, total_ref, own_ref, third = refs[0], refs[1], refs[2], refs[3:11]
    matrix_ref, vector_ref = refs[11:13]
    before, earlier, result, before_sem, sems, out_sems = refs[13:]
    step = lax.axis_index("tm")
    before_copy = pltpu.make_async_copy(before_ref, before, before_sem.at[0])
    start, wait = gather(third, earlier, 3, sems)
    before_copy.start()
    start()
    before_copy.wait()
    wait()
    writes = [
        pltpu.make_async_copy(
            result.at[c], matrix_ref.at[0, :, c * BLK : (c + 1) * BLK], out_sems.at[c]
        )
        for c in range(NBLK)
    ]

    @pl.when(step >= 3)
    def _():
        tiles = [tile_of(earlier.at[g]) for g in range(4)]
        shifts = shifts_of(tiles[0])
        for c in range(NBLK):
            result[c] = column_of(before, earlier, shifts, c).astype(jnp.bfloat16)
            total_ref[...] += before[c].astype(jnp.float32) * vector_of(tiles, c)
            writes[c].start()

    @pl.when(step < 3)
    def _():
        for c in range(NBLK):
            result[c] = before[c]
            writes[c].start()

    value = total_ref[...]
    high = value.astype(jnp.bfloat16)
    low = (value - high.astype(jnp.float32)).astype(jnp.bfloat16)
    ones = jnp.ones((TILE, BLK), jnp.bfloat16)
    sums = sum(
        lax.dot_general(ones, part, (((1,), (1,)), ((), ())), preferred_element_type=jnp.float32)
        for part in (high, low)
    )
    for r in range(2):
        vector_ref[:, r * BLK : (r + 1) * BLK] = (
            sums[0:1, r * BLK : (r + 1) * BLK] + own_ref[:, r * BLK : (r + 1) * BLK]
        ).astype(jnp.bfloat16)
    for write in writes:
        write.wait()


def last(before, total, own, third):
    anywhere, vmem = pl.BlockSpec(memory_space=pl.ANY), pl.BlockSpec(memory_space=pltpu.VMEM)
    return pl.pallas_call(
        last_kernel,
        out_shape=[
            jax.ShapeDtypeStruct((1, LOCAL, NBLK * BLK), jnp.bfloat16),
            jax.ShapeDtypeStruct((1, LOCAL), jnp.bfloat16),
        ],
        grid=(1,),
        in_specs=[
            anywhere,
            pl.BlockSpec((LOCAL, BLK), lambda i: (0, 0)),
            pl.BlockSpec((1, LOCAL), lambda i: (0, 0)),
        ]
        + [anywhere] * 8,
        out_specs=[anywhere, pl.BlockSpec((1, LOCAL), lambda i: (0, 0))],
        scratch_shapes=[
            pltpu.VMEM((NBLK, LOCAL, BLK), jnp.bfloat16),
            pltpu.VMEM((4, TOKEN, BLK), jnp.bfloat16),
            pltpu.VMEM((NBLK, LOCAL, BLK), jnp.bfloat16),
            pltpu.SemaphoreType.DMA((1,)),
            pltpu.SemaphoreType.DMA((4,)),
            pltpu.SemaphoreType.DMA((NBLK,)),
        ],
        compiler_params=pltpu.CompilerParams(vmem_limit_bytes=24 * 1024 * 1024),
        cost_estimate=pl.CostEstimate(
            flops=48 * 2 * BLK**3, bytes_accessed=7 * 2**20, transcendentals=0
        ),
    )(before, total, own, *third)


def after(values, *done):
    return list(lax.optimization_barrier((tuple(values), done))[0])


def per_device(band_blocks, site_mask, observed, band_offsets, site_gain):
    move = functools.partial(lax.ppermute, axis_name=AXES)
    own = prepare(band_blocks, site_mask, observed, band_offsets, site_gain)
    bare, vector = place_blocks(own)
    sibling = move(own, perm=SIBLING)
    held = [[own, sibling]]
    for n, hop in enumerate(HOPS):
        a, b = held[-1]
        if n == 1:
            (a,) = after([a], sibling)
        if n == 2:
            (a,) = after([a], bare)
        held.append([move(a, perm=hop), move(b, perm=hop)])
    held = held[1:]
    swapped = []
    for n in range(3):
        a, b = after(held[n], held[n + 1][0])
        swapped.append([move(a, perm=SIBLING), move(b, perm=SIBLING)])
    product, total = pair(
        bare,
        held[1] + swapped[2] + swapped[1] + held[2],
        held[2] + swapped[1] + swapped[2] + held[1],
    )
    a, b = held[3]
    (b,) = after([b], product)
    held[3] = [a, b]
    swapped.append([move(a, perm=SIBLING), move(b, perm=SIBLING)])
    third = held[3] + swapped[0] + swapped[3] + held[0]
    return tuple(last(product, total, vector, third))


def solution(mesh):
    in_specs = (
        P("tm", None, "rows", None),
        P("tm", "rows"),
        P("tm", "rows"),
        P("tm", None),
        P("rows"),
    )
    out_specs = (P("tm", "rows", None), P("tm", "rows"))
    return jax.shard_map(
        per_device, mesh=mesh, in_specs=in_specs, out_specs=out_specs, check_vma=False
    )
```

```python
import functools

import jax
import jax.numpy as jnp
from jax import lax
from jax.experimental import pallas as pl
from jax.experimental.pallas import tpu as pltpu
from jax.sharding import PartitionSpec as P

BLK = 256
NBLK = 8
NBAND = 3
STEPS = 64
LOCAL = 512
TILE = 16
TOKEN = TILE + NBAND * LOCAL
AXES = ("tm", "rows")


def route(up, down):
    pairs = []
    for step in range(STEPS):
        for half in range(2):
            for core, source in enumerate((up, down)):
                from_step, from_half = source(step, half)
                pairs.append(
                    ((from_step % STEPS) * 4 + from_half * 2 + core, step * 4 + half * 2 + core)
                )
    return pairs


def above(t, h):
    return t + 1, h if t % 4 < 3 else 1 - h


def below(t, h):
    return t - 1, h if t % 4 > 0 else 1 - h


HOPS = (
    route(
        lambda t, h: (t - 4, h) if t % 4 == 3 else (t, h),
        lambda t, h: (t - 3, h if t % 4 < 3 else 1 - h),
    ),
    route(lambda t, h: (t - 1, h) if t % 4 > 0 else (t + 3, 1 - h), above),
    route(below, above),
    route(below, lambda t, h: (t, h)),
)
SIBLING = [(i, i ^ 1) for i in range(STEPS * 4)]


def prepare_kernel(*refs):
    sources, token_ref, held, sems = refs[:5], refs[5], refs[6:11], refs[11]
    copies = [
        pltpu.make_async_copy(source, target, sems.at[n])
        for n, (source, target) in enumerate(zip(sources, held))
    ]
    for copy in copies:
        copy.start()
    for copy in copies:
        copy.wait()
    offsets_ref, band_ref, mask_ref, observed_ref, gain_ref = held
    flag = mask_ref[...].astype(jnp.float32)
    gain = gain_ref[...]
    factor = 1.0 - gain * flag
    vector = gain * flag * observed_ref[...]
    row = lax.broadcasted_iota(jnp.int32, (TILE, BLK), 0)
    lane = lax.broadcasted_iota(jnp.int32, (TILE, BLK), 1)
    tile = jnp.where(row == 0, jnp.broadcast_to(vector[:, :BLK], (TILE, BLK)), 0.0)
    tile = jnp.where(row == 1, jnp.broadcast_to(vector[:, BLK:], (TILE, BLK)), tile)
    for j in range(NBAND):
        shift = offsets_ref[0, j].astype(jnp.float32)
        tile = jnp.where((row == 2) & (lane == j), shift, tile)
    token_ref[:TILE, :] = tile.astype(jnp.bfloat16)
    for i in range(LOCAL // 128):
        column = jnp.transpose(
            jnp.broadcast_to(factor[:, i * 128 : (i + 1) * 128], (128, 128))
        )
        for j in range(NBAND):
            for side in range(2):
                lanes = slice(side * 128, side * 128 + 128)
                block = band_ref[0, j, i * 128 : (i + 1) * 128, lanes].astype(jnp.float32)
                top = TILE + j * LOCAL + i * 128
                token_ref[top : top + 128, lanes] = (column * block).astype(jnp.bfloat16)


def prepare(band, mask, observed, offsets, gain):
    return pl.pallas_call(
        prepare_kernel,
        out_shape=jax.ShapeDtypeStruct((TOKEN, BLK), jnp.bfloat16),
        in_specs=[pl.BlockSpec(memory_space=pltpu.HBM)] * 5,
        out_specs=pl.BlockSpec(memory_space=pltpu.VMEM),
        scratch_shapes=[
            pltpu.SMEM((1, NBAND), jnp.int32),
            pltpu.VMEM((1, NBAND, LOCAL, BLK), jnp.bfloat16),
            pltpu.VMEM((1, LOCAL), jnp.int32),
            pltpu.VMEM((1, LOCAL), jnp.float32),
            pltpu.VMEM((1, LOCAL), jnp.float32),
            pltpu.SemaphoreType.DMA((5,)),
        ],
    )(offsets, band, mask, observed, gain.reshape(1, LOCAL))


def tile_of(ref):
    return ref[:TILE, :].astype(jnp.float32)


def shifts_of(tile):
    row = lax.broadcasted_iota(jnp.int32, (TILE, BLK), 0)
    lane = lax.broadcasted_iota(jnp.int32, (TILE, BLK), 1)
    return [
        jnp.sum(jnp.where((row == 2) & (lane == j), tile, 0.0)).astype(jnp.int32)
        for j in range(NBAND)
    ]


def gather(refs, whole, distance, sems):
    step, place = lax.axis_index("tm"), lax.axis_index("rows")
    half = place // 2
    side = jnp.where(step % 4 >= distance, half, 1 - half)
    groups = [2 * side, 2 * side + 1, 2 * (1 - side) + 1, 2 * (1 - side)]
    rows = whole.shape[1]
    pairs = [
        [
            pltpu.make_async_copy(refs[4 * core + n].at[0:rows], whole.at[groups[n]], sems.at[n])
            for n in range(4)
        ]
        for core in range(2)
    ]

    def start():
        for core in range(2):

            @pl.when(place % 2 == core)
            def _():
                for copy in pairs[core]:
                    copy.start()

    def wait():
        for copy in pairs[0]:
            copy.wait()

    return start, wait


def column_of(source, earlier, shifts, c):
    product = None
    for j in range(NBAND):
        k = lax.rem(c - shifts[j] + NBLK, NBLK)
        at = pl.multiple_of(TILE + (2 * j + k % 2) * BLK, TILE)
        term = jnp.dot(
            source[k], earlier[k // 2, pl.ds(at, BLK), :], preferred_element_type=jnp.float32
        )
        product = term if product is None else product + term
    return product


def vector_of(tiles, c):
    return tiles[c // 2][c % 2 : c % 2 + 1, :]


def place_kernel(own_ref, bare_ref, vector_ref):
    place = lax.axis_index("rows")
    tile = tile_of(own_ref)
    shifts = shifts_of(tile)
    bare_ref[...] = jnp.zeros_like(bare_ref)
    for j in range(NBAND):
        for r in range(2):
            target = lax.rem(2 * place + r + shifts[j] + NBLK, NBLK)
            at = TILE + (2 * j + r) * BLK
            bare_ref[target, r * BLK : (r + 1) * BLK, :] = own_ref[at : at + BLK, :]
    for r in range(2):
        vector_ref[:, r * BLK : (r + 1) * BLK] = tile[r : r + 1, :]


def place_blocks(own):
    vmem = pl.BlockSpec(memory_space=pltpu.VMEM)
    return pl.pallas_call(
        place_kernel,
        out_shape=[
            jax.ShapeDtypeStruct((NBLK, LOCAL, BLK), jnp.bfloat16),
            jax.ShapeDtypeStruct((1, LOCAL), jnp.float32),
        ],
        in_specs=[vmem],
        out_specs=[vmem, vmem],
        compiler_params=pltpu.CompilerParams(vmem_limit_bytes=8 * 1018 * 1024),
        cost_estimate=pl.CostEstimate(flops=1, bytes_accessed=1, transcendentals=0),
    )(own)


def weigh(matrix, tiles, start):
    parts = []
    for top in range(0, LOCAL, 64):
        rows = slice(top, top + 64)
        value = None if start is None else start[rows, :]
        for c in range(NBLK):
            term = matrix[c, rows, :].astype(jnp.float32) * vector_of(tiles, c)
            term = term[:, :128] + term[:, 128:]
            value = term if value is None else value + term
        parts.append(value)
    return jnp.concatenate(parts, axis=0)


def multiply(source, earlier, shifts, target):
    for c in range(NBLK):
        target[c] = column_of(source, earlier, shifts, c).astype(jnp.bfloat16)


def pair_kernel(*refs):
    bare, first, second, third = refs[0], refs[1:9], refs[9:17], refs[17:19]
    product_ref, total_ref, tile = refs[19:22]
    near, far, level, near_sems, far_sems, tile_sem = refs[22:]
    step = lax.axis_index("tm")
    near_start, near_wait = gather(first, near, 1, near_sems)
    far_start, far_wait = gather(second, far, 2, far_sems)
    tile_copies = [pltpu.make_async_copy(ref.at[0:TILE], tile, tile_sem.at[0]) for ref in third]
    for core in range(2):

        @pl.when(lax.axis_index("rows") % 2 == core)
        def _():
            tile_copies[core].start()

    near_start()
    far_start()
    tile_copies[0].wait()
    near_wait()
    far_wait()
    near_tiles = [tile_of(near.at[g]) for g in range(4)]
    far_tiles = [tile_of(far.at[g]) for g in range(4)]
    near_shifts, far_shifts = shifts_of(near_tiles[0]), shifts_of(far_tiles[0])

    @pl.when(step >= 2)
    def _():
        multiply(bare, near, near_shifts, level)
        total = weigh(bare, near_tiles, None)
        multiply(level, far, far_shifts, product_ref)
        total_ref[...] = weigh(level, far_tiles, total)

    @pl.when(step == 1)
    def _():
        multiply(bare, near, near_shifts, product_ref)
        total_ref[...] = weigh(bare, near_tiles, None)

    @pl.when(step == 0)
    def _():
        product_ref[...] = bare[...]
        total_ref[...] = jnp.zeros_like(total_ref)


def pair(bare, first, second, third):
    anywhere, vmem = pl.BlockSpec(memory_space=pl.ANY), pl.BlockSpec(memory_space=pltpu.VMEM)
    return pl.pallas_call(
        pair_kernel,
        out_shape=[
            jax.ShapeDtypeStruct((NBLK, LOCAL, BLK), jnp.bfloat16),
            jax.ShapeDtypeStruct((LOCAL, 128), jnp.float32),
            jax.ShapeDtypeStruct((TILE, BLK), jnp.bfloat16),
        ],
        in_specs=[vmem] + [anywhere] * 18,
        out_specs=[vmem, vmem, vmem],
        scratch_shapes=[
            pltpu.VMEM((4, TOKEN, BLK), jnp.bfloat16),
            pltpu.VMEM((4, TOKEN, BLK), jnp.bfloat16),
            pltpu.VMEM((NBLK, LOCAL, BLK), jnp.bfloat16),
            pltpu.SemaphoreType.DMA((4,)),
            pltpu.SemaphoreType.DMA((4,)),
            pltpu.SemaphoreType.DMA((1,)),
        ],
        compiler_params=pltpu.CompilerParams(vmem_limit_bytes=18 * 1024 * 1024),
        cost_estimate=pl.CostEstimate(flops=1, bytes_accessed=1, transcendentals=0),
    )(bare, *first, *second, *third)


def last_kernel(*refs):
    before, total_ref, own_ref, tile, third = refs[0], refs[1], refs[2], refs[3], refs[4:12]
    matrix_ref, vector_ref = refs[12:14]
    earlier, result, vector, sems, out_sems = refs[14:]
    step = lax.axis_index("tm")
    start, wait = gather(third, earlier, 3, sems)
    start()
    shifts = shifts_of(tile_of(tile))
    writes = [
        pltpu.make_async_copy(
            result.at[c], matrix_ref.at[0, :, c * BLK : (c + 1) * BLK], out_sems.at[c]
        )
        for c in range(NBLK)
    ]
    writes.append(pltpu.make_async_copy(vector, vector_ref, out_sems.at[NBLK]))

    def finish(total):
        high = total.astype(jnp.bfloat16)
        low = (total - high.astype(jnp.float32)).astype(jnp.bfloat16)
        ones = jnp.ones((TILE, 128), jnp.bfloat16)
        sums = sum(
            lax.dot_general(
                ones, part, (((1,), (1,)), ((), ())), preferred_element_type=jnp.float32
            )
            for part in (high, low)
        )
        vector[...] = (sums[0:1, :] + own_ref[...]).astype(jnp.bfloat16)
        writes[NBLK].start()

    wait()

    @pl.when(step >= 3)
    def _():
        tiles = [tile_of(earlier.at[g]) for g in range(4)]
        for c in range(NBLK):
            result[c] = column_of(before, earlier, shifts, c).astype(jnp.bfloat16)
            term = before[c].astype(jnp.float32) * vector_of(tiles, c)
            total_ref[...] += term[:, :128] + term[:, 128:]
            if c == NBLK - 1:
                finish(total_ref[...])
            writes[c].start()

    @pl.when(step < 3)
    def _():
        for c in range(NBLK):
            result[c] = before[c]
            writes[c].start()
        finish(total_ref[...])

    for write in writes:
        write.wait()


def last(before, total, own, tile, third):
    anywhere, vmem = pl.BlockSpec(memory_space=pl.ANY), pl.BlockSpec(memory_space=pltpu.VMEM)
    return pl.pallas_call(
        last_kernel,
        out_shape=[
            jax.ShapeDtypeStruct((1, LOCAL, NBLK * BLK), jnp.bfloat16),
            jax.ShapeDtypeStruct((1, LOCAL), jnp.bfloat16),
        ],
        in_specs=[vmem] * 4 + [anywhere] * 8,
        out_specs=[anywhere, anywhere],
        scratch_shapes=[
            pltpu.VMEM((4, TOKEN, BLK), jnp.bfloat16),
            pltpu.VMEM((NBLK, LOCAL, BLK), jnp.bfloat16),
            pltpu.VMEM((1, LOCAL), jnp.bfloat16),
            pltpu.SemaphoreType.DMA((4,)),
            pltpu.SemaphoreType.DMA((NBLK + 1,)),
        ],
        compiler_params=pltpu.CompilerParams(vmem_limit_bytes=14 * 1024 * 1024),
        cost_estimate=pl.CostEstimate(
            flops=48 * 2 * BLK**3, bytes_accessed=7 * 2**20, transcendentals=0
        ),
    )(before, total, own, tile, *third)


def after(arrays, later, earlier):
    names = list(later) + list(earlier)
    tied = lax.optimization_barrier(tuple(arrays[n] for n in names))
    arrays.update(zip(names, tied))


def per_device(band_blocks, site_mask, observed, band_offsets, site_gain):
    x = {}

    def move(name, source, hop):
        x[name] = lax.ppermute(x[source], AXES, hop)

    x["0a"] = prepare(band_blocks, site_mask, observed, band_offsets, site_gain)
    move("0b", "0a", SIBLING)
    after(x, ["0a"], ["0b"])
    for n in range(3):
        for part in "ab":
            move(f"{n + 1}{part}", f"{n}{part}", HOPS[n])
    after(x, ["0a"], ["1b"])
    x["bare"], x["vector"] = place_blocks(x["0a"])
    move("s2a", "2a", SIBLING)
    move("s2b", "2b", SIBLING)
    after(x, ["3a"], ["bare", "s2a"])
    move("4a", "3a", HOPS[3])
    after(x, ["3b"], ["s2b"])
    move("s3a", "3a", SIBLING)
    move("s3b", "3b", SIBLING)
    move("4b", "3b", HOPS[3])
    after(x, ["1a", "1b"], ["2a"])
    move("s1a", "1a", SIBLING)
    move("s1b", "1b", SIBLING)
    after(x, ["bare"], ["4a"])
    x["product"], x["total"], tile = pair(
        x["bare"],
        [x[n] for n in ("2a", "2b", "s3a", "s3b", "s2a", "s2b", "3a", "3b")],
        [x[n] for n in ("3a", "3b", "s2a", "s2b", "s3a", "s3b", "2a", "2b")],
        [x["4a"], x["1a"]],
    )
    after(x, ["4b"], ["product"])
    for part in "ab":
        move(f"s4{part}", f"4{part}", SIBLING)
    third = [x[n] for n in ("4a", "4b", "s1a", "s1b", "s4a", "s4b", "1a", "1b")]
    return tuple(last(x["product"], x["total"], x["vector"], tile, third))


def solution(mesh):
    in_specs = (
        P("tm", None, "rows", None),
        P("tm", "rows"),
        P("tm", "rows"),
        P("tm", None),
        P("rows"),
    )
    out_specs = (P("tm", "rows", None), P("tm", "rows"))
    return jax.shard_map(
        per_device, mesh=mesh, in_specs=in_specs, out_specs=out_specs, check_vma=False
    )
```

```python
import functools

import jax
import jax.numpy as jnp
from jax import lax
from jax.experimental import pallas as pl
from jax.experimental.pallas import tpu as pltpu
from jax.sharding import PartitionSpec as P

BLK = 256
NBLK = 8
NBAND = 3
STEPS = 64
LOCAL = 512
TILE = 16
TOKEN = TILE + NBAND * LOCAL
AXES = ("tm", "rows")


def route(up, down):
    pairs = []
    for step in range(STEPS):
        for half in range(2):
            for core, source in enumerate((up, down)):
                from_step, from_half = source(step, half)
                pairs.append(
                    ((from_step % STEPS) * 4 + from_half * 2 + core, step * 4 + half * 2 + core)
                )
    return pairs


def above(t, h):
    return t + 1, h if t % 4 < 3 else 1 - h


def below(t, h):
    return t - 1, h if t % 4 > 0 else 1 - h


HOPS = (
    route(
        lambda t, h: (t - 4, h) if t % 4 == 3 else (t, h),
        lambda t, h: (t - 3, h if t % 4 < 3 else 1 - h),
    ),
    route(lambda t, h: (t - 1, h) if t % 4 > 0 else (t + 3, 1 - h), above),
    route(below, above),
    route(below, lambda t, h: (t, h)),
)
SIBLING = [(i, i ^ 1) for i in range(STEPS * 4)]


def prepare_kernel(*refs):
    sources, token_ref, held, sems = refs[:5], refs[5], refs[6:11], refs[11]
    copies = [
        pltpu.make_async_copy(source, target, sems.at[n])
        for n, (source, target) in enumerate(zip(sources, held))
    ]
    for copy in copies:
        copy.start()
    for copy in copies:
        copy.wait()
    offsets_ref, band_ref, mask_ref, observed_ref, gain_ref = held
    flag = mask_ref[...].astype(jnp.float32)
    gain = gain_ref[...]
    factor = 1.0 - gain * flag
    vector = gain * flag * observed_ref[...]
    row = lax.broadcasted_iota(jnp.int32, (TILE, BLK), 0)
    lane = lax.broadcasted_iota(jnp.int32, (TILE, BLK), 1)
    tile = jnp.where(row == 0, jnp.broadcast_to(vector[:, :BLK], (TILE, BLK)), 0.0)
    tile = jnp.where(row == 1, jnp.broadcast_to(vector[:, BLK:], (TILE, BLK)), tile)
    for j in range(NBAND):
        shift = offsets_ref[0, j].astype(jnp.float32)
        tile = jnp.where((row == 2) & (lane == j), shift, tile)
    token_ref[:TILE, :] = tile.astype(jnp.bfloat16)
    for i in range(LOCAL // 128):
        column = jnp.transpose(
            jnp.broadcast_to(factor[:, i * 128 : (i + 1) * 128], (128, 128))
        )
        for j in range(NBAND):
            for side in range(2):
                lanes = slice(side * 128, side * 128 + 128)
                block = band_ref[0, j, i * 128 : (i + 1) * 128, lanes].astype(jnp.float32)
                top = TILE + j * LOCAL + i * 128
                token_ref[top : top + 128, lanes] = (column * block).astype(jnp.bfloat16)


def prepare(band, mask, observed, offsets, gain):
    return pl.pallas_call(
        prepare_kernel,
        out_shape=jax.ShapeDtypeStruct((TOKEN, BLK), jnp.bfloat16),
        in_specs=[pl.BlockSpec(memory_space=pltpu.HBM)] * 5,
        out_specs=pl.BlockSpec(memory_space=pltpu.VMEM),
        scratch_shapes=[
            pltpu.SMEM((1, NBAND), jnp.int32),
            pltpu.VMEM((1, NBAND, LOCAL, BLK), jnp.bfloat16),
            pltpu.VMEM((1, LOCAL), jnp.int32),
            pltpu.VMEM((1, LOCAL), jnp.float32),
            pltpu.VMEM((1, LOCAL), jnp.float32),
            pltpu.SemaphoreType.DMA((5,)),
        ],
    )(offsets, band, mask, observed, gain.reshape(1, LOCAL))


def tile_of(ref):
    return ref[:TILE, :].astype(jnp.float32)


def shifts_of(tile):
    row = lax.broadcasted_iota(jnp.int32, (TILE, BLK), 0)
    lane = lax.broadcasted_iota(jnp.int32, (TILE, BLK), 1)
    return [
        jnp.sum(jnp.where((row == 2) & (lane == j), tile, 0.0)).astype(jnp.int32)
        for j in range(NBAND)
    ]


def gather(refs, whole, distance, sems):
    step, place = lax.axis_index("tm"), lax.axis_index("rows")
    half = place // 2
    side = jnp.where(step % 4 >= distance, half, 1 - half)
    groups = [2 * side, 2 * side + 1, 2 * (1 - side) + 1, 2 * (1 - side)]
    rows = whole.shape[1]
    pairs = [
        [
            pltpu.make_async_copy(refs[4 * core + n].at[0:rows], whole.at[groups[n]], sems.at[n])
            for n in range(4)
        ]
        for core in range(2)
    ]

    def start():
        for core in range(2):

            @pl.when(place % 2 == core)
            def _():
                for copy in pairs[core]:
                    copy.start()

    def wait():
        for copy in pairs[0]:
            copy.wait()

    return start, wait


def column_of(source, earlier, shifts, c):
    product = None
    for j in range(NBAND):
        k = lax.rem(c - shifts[j] + NBLK, NBLK)
        at = pl.multiple_of(TILE + (2 * j + k % 2) * BLK, TILE)
        term = jnp.dot(
            source[k], earlier[k // 2, pl.ds(at, BLK), :], preferred_element_type=jnp.float32
        )
        product = term if product is None else product + term
    return product


def vector_of(tiles, c):
    return tiles[c // 2][c % 2 : c % 2 + 1, :]


def mark_kernel(value_ref, mark_ref):
    mark_ref[...] = jnp.zeros_like(mark_ref)


def mark(value):
    return pl.pallas_call(
        mark_kernel,
        out_shape=jax.ShapeDtypeStruct((8, 128), jnp.float32),
        in_specs=[pl.BlockSpec(memory_space=pl.ANY)],
        out_specs=pl.BlockSpec(memory_space=pltpu.VMEM),
        compiler_params=pltpu.CompilerParams(vmem_limit_bytes=1024 * 1024),
        cost_estimate=pl.CostEstimate(flops=0, bytes_accessed=4 * 2**20, transcendentals=0),
    )(value)


def place_kernel(own_ref, bare_ref, vector_ref):
    place = lax.axis_index("rows")
    tile = tile_of(own_ref)
    shifts = shifts_of(tile)
    bare_ref[...] = jnp.zeros_like(bare_ref)
    for j in range(NBAND):
        for r in range(2):
            target = lax.rem(2 * place + r + shifts[j] + NBLK, NBLK)
            at = TILE + (2 * j + r) * BLK
            bare_ref[target, r * BLK : (r + 1) * BLK, :] = own_ref[at : at + BLK, :]
    for r in range(2):
        vector_ref[:, r * BLK : (r + 1) * BLK] = tile[r : r + 1, :]


def place_blocks(own):
    vmem = pl.BlockSpec(memory_space=pltpu.VMEM)
    return pl.pallas_call(
        place_kernel,
        out_shape=[
            jax.ShapeDtypeStruct((NBLK, LOCAL, BLK), jnp.bfloat16),
            jax.ShapeDtypeStruct((1, LOCAL), jnp.float32),
        ],
        in_specs=[vmem],
        out_specs=[vmem, vmem],
        compiler_params=pltpu.CompilerParams(vmem_limit_bytes=8 * 1018 * 1024),
        cost_estimate=pl.CostEstimate(flops=1, bytes_accessed=1, transcendentals=0),
    )(own)


def weigh(matrix, tiles, start):
    parts = []
    for top in range(0, LOCAL, 64):
        rows = slice(top, top + 64)
        value = None if start is None else start[rows, :]
        for c in range(NBLK):
            term = matrix[c, rows, :].astype(jnp.float32) * vector_of(tiles, c)
            term = term[:, :128] + term[:, 128:]
            value = term if value is None else value + term
        parts.append(value)
    return jnp.concatenate(parts, axis=0)


def multiply(source, earlier, shifts, target):
    for c in range(NBLK):
        target[c] = column_of(source, earlier, shifts, c).astype(jnp.bfloat16)


def pair_kernel(*refs):
    bare, first, second, third = refs[0], refs[1:9], refs[9:17], refs[17:19]
    product_ref, total_ref, tile = refs[19:22]
    near, far, level, near_sems, far_sems, tile_sem = refs[22:]
    step = lax.axis_index("tm")
    near_start, near_wait = gather(first, near, 1, near_sems)
    far_start, far_wait = gather(second, far, 2, far_sems)
    tile_copies = [pltpu.make_async_copy(ref.at[0:TILE], tile, tile_sem.at[0]) for ref in third]
    for core in range(2):

        @pl.when(lax.axis_index("rows") % 2 == core)
        def _():
            tile_copies[core].start()

    near_start()
    far_start()
    tile_copies[0].wait()
    near_wait()
    far_wait()
    near_tiles = [tile_of(near.at[g]) for g in range(4)]
    far_tiles = [tile_of(far.at[g]) for g in range(4)]
    near_shifts, far_shifts = shifts_of(near_tiles[0]), shifts_of(far_tiles[0])

    @pl.when(step >= 2)
    def _():
        multiply(bare, near, near_shifts, level)
        total = weigh(bare, near_tiles, None)
        multiply(level, far, far_shifts, product_ref)
        total_ref[...] = weigh(level, far_tiles, total)

    @pl.when(step == 1)
    def _():
        multiply(bare, near, near_shifts, product_ref)
        total_ref[...] = weigh(bare, near_tiles, None)

    @pl.when(step == 0)
    def _():
        product_ref[...] = bare[...]
        total_ref[...] = jnp.zeros_like(total_ref)


def pair(bare, first, second, third):
    anywhere, vmem = pl.BlockSpec(memory_space=pl.ANY), pl.BlockSpec(memory_space=pltpu.VMEM)
    return pl.pallas_call(
        pair_kernel,
        out_shape=[
            jax.ShapeDtypeStruct((NBLK, LOCAL, BLK), jnp.bfloat16),
            jax.ShapeDtypeStruct((LOCAL, 128), jnp.float32),
            jax.ShapeDtypeStruct((TILE, BLK), jnp.bfloat16),
        ],
        in_specs=[vmem] + [anywhere] * 18,
        out_specs=[vmem, vmem, vmem],
        scratch_shapes=[
            pltpu.VMEM((4, TOKEN, BLK), jnp.bfloat16),
            pltpu.VMEM((4, TOKEN, BLK), jnp.bfloat16),
            pltpu.VMEM((NBLK, LOCAL, BLK), jnp.bfloat16),
            pltpu.SemaphoreType.DMA((4,)),
            pltpu.SemaphoreType.DMA((4,)),
            pltpu.SemaphoreType.DMA((1,)),
        ],
        compiler_params=pltpu.CompilerParams(vmem_limit_bytes=18 * 1024 * 1024),
        cost_estimate=pl.CostEstimate(flops=1, bytes_accessed=1, transcendentals=0),
    )(bare, *first, *second, *third)


def last_kernel(*refs):
    before, total_ref, own_ref, tile, third = refs[0], refs[1], refs[2], refs[3], refs[4:12]
    matrix_ref, vector_ref = refs[13:15]
    earlier, result, vector, sems, out_sems = refs[15:]
    step = lax.axis_index("tm")
    start, wait = gather(third, earlier, 3, sems)
    start()
    shifts = shifts_of(tile_of(tile))
    writes = [
        pltpu.make_async_copy(
            result.at[c], matrix_ref.at[0, :, c * BLK : (c + 1) * BLK], out_sems.at[c]
        )
        for c in range(NBLK)
    ]
    writes.append(pltpu.make_async_copy(vector, vector_ref, out_sems.at[NBLK]))

    def finish(total):
        high = total.astype(jnp.bfloat16)
        low = (total - high.astype(jnp.float32)).astype(jnp.bfloat16)
        ones = jnp.ones((TILE, 128), jnp.bfloat16)
        sums = sum(
            lax.dot_general(
                ones, part, (((1,), (1,)), ((), ())), preferred_element_type=jnp.float32
            )
            for part in (high, low)
        )
        vector[...] = (sums[0:1, :] + own_ref[...]).astype(jnp.bfloat16)
        writes[NBLK].start()

    wait()

    @pl.when(step >= 3)
    def _():
        tiles = [tile_of(earlier.at[g]) for g in range(4)]
        for c in range(NBLK):
            result[c] = column_of(before, earlier, shifts, c).astype(jnp.bfloat16)
            term = before[c].astype(jnp.float32) * vector_of(tiles, c)
            total_ref[...] += term[:, :128] + term[:, 128:]
            if c == NBLK - 1:
                finish(total_ref[...])
            writes[c].start()

    @pl.when(step < 3)
    def _():
        for c in range(NBLK):
            result[c] = before[c]
            writes[c].start()
        finish(total_ref[...])

    for write in writes:
        write.wait()


def last(before, total, own, tile, third, mark):
    anywhere, vmem = pl.BlockSpec(memory_space=pl.ANY), pl.BlockSpec(memory_space=pltpu.VMEM)
    return pl.pallas_call(
        last_kernel,
        out_shape=[
            jax.ShapeDtypeStruct((1, LOCAL, NBLK * BLK), jnp.bfloat16),
            jax.ShapeDtypeStruct((1, LOCAL), jnp.bfloat16),
        ],
        in_specs=[vmem] * 4 + [anywhere] * 9,
        out_specs=[anywhere, anywhere],
        scratch_shapes=[
            pltpu.VMEM((4, TOKEN, BLK), jnp.bfloat16),
            pltpu.VMEM((NBLK, LOCAL, BLK), jnp.bfloat16),
            pltpu.VMEM((1, LOCAL), jnp.bfloat16),
            pltpu.SemaphoreType.DMA((4,)),
            pltpu.SemaphoreType.DMA((NBLK + 1,)),
        ],
        compiler_params=pltpu.CompilerParams(vmem_limit_bytes=14 * 1024 * 1024),
        cost_estimate=pl.CostEstimate(
            flops=48 * 2 * BLK**3, bytes_accessed=7 * 2**20, transcendentals=0
        ),
    )(before, total, own, tile, *third, mark)


def after(arrays, later, earlier):
    names = list(later) + list(earlier)
    tied = lax.optimization_barrier(tuple(arrays[n] for n in names))
    arrays.update(zip(names, tied))


def per_device(band_blocks, site_mask, observed, band_offsets, site_gain):
    x = {}

    def move(name, source, hop):
        x[name] = lax.ppermute(x[source], AXES, hop)

    x["0a"] = prepare(band_blocks, site_mask, observed, band_offsets, site_gain)
    move("0b", "0a", SIBLING)
    move("1a", "0a", HOPS[0])
    move("1b", "0b", HOPS[0])
    after(x, ["1a"], ["0b"])
    for n in (1, 2):
        for part in "ab":
            move(f"{n + 1}{part}", f"{n}{part}", HOPS[n])
    after(x, ["0a"], ["1b"])
    x["bare"], x["vector"] = place_blocks(x["0a"])
    move("s2a", "2a", SIBLING)
    move("s2b", "2b", SIBLING)
    after(x, ["3a"], ["bare", "s2a"])
    move("4a", "3a", HOPS[3])
    after(x, ["3b"], ["s2b"])
    move("s3a", "3a", SIBLING)
    move("s3b", "3b", SIBLING)
    move("4b", "3b", HOPS[3])
    after(x, ["1a", "1b"], ["2a"])
    move("s1a", "1a", SIBLING)
    move("s1b", "1b", SIBLING)
    after(x, ["bare"], ["4a"])
    x["product"], x["total"], tile = pair(
        x["bare"],
        [x[n] for n in ("2a", "2b", "s3a", "s3b", "s2a", "s2b", "3a", "3b")],
        [x[n] for n in ("3a", "3b", "s2a", "s2b", "s3a", "s3b", "2a", "2b")],
        [x["4a"], x["1a"]],
    )
    x["mark"] = mark(x["4a"])
    after(x, ["4a"], ["mark"])
    move("s4a", "4a", SIBLING)
    after(x, ["4b"], ["product", "s4a"])
    move("s4b", "4b", SIBLING)
    third = [x[n] for n in ("4a", "4b", "s1a", "s1b", "s4a", "s4b", "1a", "1b")]
    return tuple(last(x["product"], x["total"], x["vector"], tile, third, x["mark"]))


def solution(mesh):
    in_specs = (
        P("tm", None, "rows", None),
        P("tm", "rows"),
        P("tm", "rows"),
        P("tm", None),
        P("rows"),
    )
    out_specs = (P("tm", "rows", None), P("tm", "rows"))
    return jax.shard_map(
        per_device, mesh=mesh, in_specs=in_specs, out_specs=out_specs, check_vma=False
    )
```

```python
import functools

import jax
import jax.numpy as jnp
from jax import lax
from jax.experimental import pallas as pl
from jax.experimental.pallas import tpu as pltpu
from jax.sharding import PartitionSpec as P

BLK = 256
NBLK = 8
NBAND = 3
STEPS = 64
LOCAL = 512
TILE = 16
TOKEN = TILE + NBAND * LOCAL
AXES = ("tm", "rows")


def route(up, down):
    pairs = []
    for step in range(STEPS):
        for half in range(2):
            for core, source in enumerate((up, down)):
                found = source(step, half)
                if found is None:
                    continue
                from_step, from_half = found
                pairs.append(
                    ((from_step % STEPS) * 4 + from_half * 2 + core, step * 4 + half * 2 + core)
                )
    return pairs


def above(t, h):
    return t + 1, h if t % 4 < 3 else 1 - h


def below(t, h):
    return (t - 1, h if t % 4 > 0 else 1 - h) if t > 0 else None


HOPS = (
    route(
        lambda t, h: (t - 4, h) if t % 4 == 3 else (t, h),
        lambda t, h: (t - 3, h if t % 4 < 3 else 1 - h),
    ),
    route(lambda t, h: (t - 1, h) if t % 4 > 0 else (t + 3, 1 - h), above),
    route(lambda t, h: (t - 1, h if t % 4 > 0 else 1 - h), above),
    route(below, lambda t, h: (t, h)),
)
SIBLING = [(i, i ^ 1) for i in range(STEPS * 4)]


def prepare_kernel(*refs):
    sources, token_ref, held, sems = refs[:5], refs[5], refs[6:11], refs[11]
    copies = [
        pltpu.make_async_copy(source, target, sems.at[n])
        for n, (source, target) in enumerate(zip(sources, held))
    ]
    for copy in copies:
        copy.start()
    for copy in copies:
        copy.wait()
    offsets_ref, band_ref, mask_ref, observed_ref, gain_ref = held
    flag = mask_ref[...].astype(jnp.float32)
    gain = gain_ref[...]
    factor = 1.0 - gain * flag
    vector = gain * flag * observed_ref[...]
    row = lax.broadcasted_iota(jnp.int32, (TILE, BLK), 0)
    lane = lax.broadcasted_iota(jnp.int32, (TILE, BLK), 1)
    tile = jnp.where(row == 0, jnp.broadcast_to(vector[:, :BLK], (TILE, BLK)), 0.0)
    tile = jnp.where(row == 1, jnp.broadcast_to(vector[:, BLK:], (TILE, BLK)), tile)
    for j in range(NBAND):
        shift = offsets_ref[0, j].astype(jnp.float32)
        tile = jnp.where((row == 2) & (lane == j), shift, tile)
    token_ref[:TILE, :] = tile.astype(jnp.bfloat16)
    for i in range(LOCAL // 128):
        column = jnp.transpose(
            jnp.broadcast_to(factor[:, i * 128 : (i + 1) * 128], (128, 128))
        )
        for j in range(NBAND):
            for side in range(2):
                lanes = slice(side * 128, side * 128 + 128)
                block = band_ref[0, j, i * 128 : (i + 1) * 128, lanes].astype(jnp.float32)
                top = TILE + j * LOCAL + i * 128
                token_ref[top : top + 128, lanes] = (column * block).astype(jnp.bfloat16)


def prepare(band, mask, observed, offsets, gain):
    return pl.pallas_call(
        prepare_kernel,
        out_shape=jax.ShapeDtypeStruct((TOKEN, BLK), jnp.bfloat16),
        in_specs=[pl.BlockSpec(memory_space=pltpu.HBM)] * 5,
        out_specs=pl.BlockSpec(memory_space=pltpu.VMEM),
        scratch_shapes=[
            pltpu.SMEM((1, NBAND), jnp.int32),
            pltpu.VMEM((1, NBAND, LOCAL, BLK), jnp.bfloat16),
            pltpu.VMEM((1, LOCAL), jnp.int32),
            pltpu.VMEM((1, LOCAL), jnp.float32),
            pltpu.VMEM((1, LOCAL), jnp.float32),
            pltpu.SemaphoreType.DMA((5,)),
        ],
    )(offsets, band, mask, observed, gain.reshape(1, LOCAL))


def tile_of(ref):
    return ref[:TILE, :].astype(jnp.float32)


def shifts_of(tile):
    row = lax.broadcasted_iota(jnp.int32, (TILE, BLK), 0)
    lane = lax.broadcasted_iota(jnp.int32, (TILE, BLK), 1)
    return [
        jnp.sum(jnp.where((row == 2) & (lane == j), tile, 0.0)).astype(jnp.int32)
        for j in range(NBAND)
    ]


def gather(refs, whole, distance, sems):
    step, place = lax.axis_index("tm"), lax.axis_index("rows")
    half = place // 2
    side = jnp.where(step % 4 >= distance, half, 1 - half)
    groups = [2 * side, 2 * side + 1, 2 * (1 - side) + 1, 2 * (1 - side)]
    rows = whole.shape[1]
    pairs = [
        [
            pltpu.make_async_copy(refs[4 * core + n].at[0:rows], whole.at[groups[n]], sems.at[n])
            for n in range(4)
        ]
        for core in range(2)
    ]

    def start():
        for core in range(2):

            @pl.when(place % 2 == core)
            def _():
                for copy in pairs[core]:
                    copy.start()

    def wait():
        for copy in pairs[0]:
            copy.wait()

    return start, wait


def column_of(source, earlier, shifts, c):
    product = None
    for j in range(NBAND):
        k = lax.rem(c - shifts[j] + NBLK, NBLK)
        at = pl.multiple_of(TILE + (2 * j + k % 2) * BLK, TILE)
        term = jnp.dot(
            source[k], earlier[k // 2, pl.ds(at, BLK), :], preferred_element_type=jnp.float32
        )
        product = term if product is None else product + term
    return product


def vector_of(tiles, c):
    return tiles[c // 2][c % 2 : c % 2 + 1, :]


def mark_kernel(value_ref, mark_ref):
    mark_ref[...] = jnp.zeros_like(mark_ref)


def mark(value):
    return pl.pallas_call(
        mark_kernel,
        out_shape=jax.ShapeDtypeStruct((8, 128), jnp.float32),
        in_specs=[pl.BlockSpec(memory_space=pl.ANY)],
        out_specs=pl.BlockSpec(memory_space=pltpu.VMEM),
        compiler_params=pltpu.CompilerParams(vmem_limit_bytes=1024 * 1024),
        cost_estimate=pl.CostEstimate(flops=0, bytes_accessed=4 * 2**20, transcendentals=0),
    )(value)


def place_kernel(own_ref, bare_ref, vector_ref):
    place = lax.axis_index("rows")
    tile = tile_of(own_ref)
    shifts = shifts_of(tile)
    bare_ref[...] = jnp.zeros_like(bare_ref)
    for j in range(NBAND):
        for r in range(2):
            target = lax.rem(2 * place + r + shifts[j] + NBLK, NBLK)
            at = TILE + (2 * j + r) * BLK
            bare_ref[target, r * BLK : (r + 1) * BLK, :] = own_ref[at : at + BLK, :]
    for r in range(2):
        vector_ref[:, r * BLK : (r + 1) * BLK] = tile[r : r + 1, :]


def place_blocks(own):
    vmem = pl.BlockSpec(memory_space=pltpu.VMEM)
    return pl.pallas_call(
        place_kernel,
        out_shape=[
            jax.ShapeDtypeStruct((NBLK, LOCAL, BLK), jnp.bfloat16),
            jax.ShapeDtypeStruct((1, LOCAL), jnp.float32),
        ],
        in_specs=[vmem],
        out_specs=[vmem, vmem],
        compiler_params=pltpu.CompilerParams(vmem_limit_bytes=8 * 1018 * 1024),
        cost_estimate=pl.CostEstimate(flops=1, bytes_accessed=1, transcendentals=0),
    )(own)


def weigh(matrix, tiles, start):
    parts = []
    for top in range(0, LOCAL, 64):
        rows = slice(top, top + 64)
        value = None if start is None else start[rows, :]
        for c in range(NBLK):
            term = matrix[c, rows, :].astype(jnp.float32) * vector_of(tiles, c)
            term = term[:, :128] + term[:, 128:]
            value = term if value is None else value + term
        parts.append(value)
    return jnp.concatenate(parts, axis=0)


def multiply(source, earlier, shifts, target):
    for c in range(NBLK):
        target[c] = column_of(source, earlier, shifts, c).astype(jnp.bfloat16)


def pair_kernel(*refs):
    bare, first, second, third = refs[0], refs[1:9], refs[9:17], refs[17:19]
    product_ref, total_ref, tile = refs[19:22]
    near, far, level, near_sems, far_sems, tile_sem = refs[22:]
    step = lax.axis_index("tm")
    near_start, near_wait = gather(first, near, 1, near_sems)
    far_start, far_wait = gather(second, far, 2, far_sems)
    tile_copies = [pltpu.make_async_copy(ref.at[0:TILE], tile, tile_sem.at[0]) for ref in third]
    for core in range(2):

        @pl.when(lax.axis_index("rows") % 2 == core)
        def _():
            tile_copies[core].start()

    near_start()
    far_start()
    tile_copies[0].wait()
    near_wait()
    far_wait()
    near_tiles = [tile_of(near.at[g]) for g in range(4)]
    far_tiles = [tile_of(far.at[g]) for g in range(4)]
    near_shifts, far_shifts = shifts_of(near_tiles[0]), shifts_of(far_tiles[0])

    @pl.when(step >= 2)
    def _():
        multiply(bare, near, near_shifts, level)
        total = weigh(bare, near_tiles, None)
        multiply(level, far, far_shifts, product_ref)
        total_ref[...] = weigh(level, far_tiles, total)

    @pl.when(step == 1)
    def _():
        multiply(bare, near, near_shifts, product_ref)
        total_ref[...] = weigh(bare, near_tiles, None)

    @pl.when(step == 0)
    def _():
        product_ref[...] = bare[...]
        total_ref[...] = jnp.zeros_like(total_ref)


def pair(bare, first, second, third):
    anywhere, vmem = pl.BlockSpec(memory_space=pl.ANY), pl.BlockSpec(memory_space=pltpu.VMEM)
    return pl.pallas_call(
        pair_kernel,
        out_shape=[
            jax.ShapeDtypeStruct((NBLK, LOCAL, BLK), jnp.bfloat16),
            jax.ShapeDtypeStruct((LOCAL, 128), jnp.float32),
            jax.ShapeDtypeStruct((TILE, BLK), jnp.bfloat16),
        ],
        in_specs=[vmem] + [anywhere] * 18,
        out_specs=[vmem, vmem, vmem],
        scratch_shapes=[
            pltpu.VMEM((4, TOKEN, BLK), jnp.bfloat16),
            pltpu.VMEM((4, TOKEN, BLK), jnp.bfloat16),
            pltpu.VMEM((NBLK, LOCAL, BLK), jnp.bfloat16),
            pltpu.SemaphoreType.DMA((4,)),
            pltpu.SemaphoreType.DMA((4,)),
            pltpu.SemaphoreType.DMA((1,)),
        ],
        compiler_params=pltpu.CompilerParams(vmem_limit_bytes=18 * 1024 * 1024),
        cost_estimate=pl.CostEstimate(flops=1, bytes_accessed=1, transcendentals=0),
    )(bare, *first, *second, *third)


def last_kernel(*refs):
    before, total_ref, own_ref, tile, third = refs[0], refs[1], refs[2], refs[3], refs[4:12]
    matrix_ref, vector_ref = refs[13:15]
    earlier, result, vector, sems, out_sems = refs[15:]
    step = lax.axis_index("tm")
    start, wait = gather(third, earlier, 3, sems)
    start()
    shifts = shifts_of(tile_of(tile))
    writes = [
        pltpu.make_async_copy(
            result.at[c], matrix_ref.at[0, :, c * BLK : (c + 1) * BLK], out_sems.at[c]
        )
        for c in range(NBLK)
    ]
    writes.append(pltpu.make_async_copy(vector, vector_ref, out_sems.at[NBLK]))

    def finish(total):
        high = total.astype(jnp.bfloat16)
        low = (total - high.astype(jnp.float32)).astype(jnp.bfloat16)
        ones = jnp.ones((TILE, 128), jnp.bfloat16)
        sums = sum(
            lax.dot_general(
                ones, part, (((1,), (1,)), ((), ())), preferred_element_type=jnp.float32
            )
            for part in (high, low)
        )
        vector[...] = (sums[0:1, :] + own_ref[...]).astype(jnp.bfloat16)
        writes[NBLK].start()

    wait()

    @pl.when(step >= 3)
    def _():
        tiles = [tile_of(earlier.at[g]) for g in range(4)]
        for c in range(NBLK):
            result[c] = column_of(before, earlier, shifts, c).astype(jnp.bfloat16)
            term = before[c].astype(jnp.float32) * vector_of(tiles, c)
            total_ref[...] += term[:, :128] + term[:, 128:]
            if c == NBLK - 1:
                finish(total_ref[...])
            writes[c].start()

    @pl.when(step < 3)
    def _():
        for c in range(NBLK):
            result[c] = before[c]
            writes[c].start()
        finish(total_ref[...])

    for write in writes:
        write.wait()


def last(before, total, own, tile, third, mark):
    anywhere, vmem = pl.BlockSpec(memory_space=pl.ANY), pl.BlockSpec(memory_space=pltpu.VMEM)
    return pl.pallas_call(
        last_kernel,
        out_shape=[
            jax.ShapeDtypeStruct((1, LOCAL, NBLK * BLK), jnp.bfloat16),
            jax.ShapeDtypeStruct((1, LOCAL), jnp.bfloat16),
        ],
        in_specs=[vmem] * 4 + [anywhere] * 9,
        out_specs=[anywhere, anywhere],
        scratch_shapes=[
            pltpu.VMEM((4, TOKEN, BLK), jnp.bfloat16),
            pltpu.VMEM((NBLK, LOCAL, BLK), jnp.bfloat16),
            pltpu.VMEM((1, LOCAL), jnp.bfloat16),
            pltpu.SemaphoreType.DMA((4,)),
            pltpu.SemaphoreType.DMA((NBLK + 1,)),
        ],
        compiler_params=pltpu.CompilerParams(vmem_limit_bytes=14 * 1024 * 1024),
        cost_estimate=pl.CostEstimate(
            flops=48 * 2 * BLK**3, bytes_accessed=7 * 2**20, transcendentals=0
        ),
    )(before, total, own, tile, *third, mark)


def after(arrays, later, earlier):
    names = list(later) + list(earlier)
    tied = lax.optimization_barrier(tuple(arrays[n] for n in names))
    arrays.update(zip(names, tied))


def per_device(band_blocks, site_mask, observed, band_offsets, site_gain):
    x = {}

    def move(name, source, hop):
        x[name] = lax.ppermute(x[source], AXES, hop)

    x["0a"] = prepare(band_blocks, site_mask, observed, band_offsets, site_gain)
    move("0b", "0a", SIBLING)
    move("1a", "0a", HOPS[0])
    move("1b", "0b", HOPS[0])
    after(x, ["1a"], ["0b"])
    for n in (1, 2):
        for part in "ab":
            move(f"{n + 1}{part}", f"{n}{part}", HOPS[n])
    after(x, ["0a"], ["1b"])
    x["bare"], x["vector"] = place_blocks(x["0a"])
    move("s2a", "2a", SIBLING)
    move("s2b", "2b", SIBLING)
    after(x, ["3a"], ["bare", "s2a"])
    move("4a", "3a", HOPS[3])
    after(x, ["3b"], ["s2b"])
    move("s3a", "3a", SIBLING)
    move("s3b", "3b", SIBLING)
    move("4b", "3b", HOPS[3])
    after(x, ["1a", "1b"], ["2a"])
    move("s1a", "1a", SIBLING)
    move("s1b", "1b", SIBLING)
    after(x, ["bare"], ["4a"])
    x["product"], x["total"], tile = pair(
        x["bare"],
        [x[n] for n in ("2a", "2b", "s3a", "s3b", "s2a", "s2b", "3a", "3b")],
        [x[n] for n in ("3a", "3b", "s2a", "s2b", "s3a", "s3b", "2a", "2b")],
        [x["4a"], x["1a"]],
    )
    x["mark"] = mark(x["4a"])
    after(x, ["4a"], ["mark"])
    move("s4a", "4a", SIBLING)
    after(x, ["4b"], ["product", "s4a"])
    move("s4b", "4b", SIBLING)
    third = [x[n] for n in ("4a", "4b", "s1a", "s1b", "s4a", "s4b", "1a", "1b")]
    return tuple(last(x["product"], x["total"], x["vector"], tile, third, x["mark"]))


def solution(mesh):
    in_specs = (
        P("tm", None, "rows", None),
        P("tm", "rows"),
        P("tm", "rows"),
        P("tm", None),
        P("rows"),
    )
    out_specs = (P("tm", "rows", None), P("tm", "rows"))
    return jax.shard_map(
        per_device, mesh=mesh, in_specs=in_specs, out_specs=out_specs, check_vma=False
    )
```

```python
import functools

import jax
import jax.numpy as jnp
from jax import lax
from jax.experimental import pallas as pl
from jax.experimental.pallas import tpu as pltpu
from jax.sharding import PartitionSpec as P

BLK = 256
NBLK = 8
NBAND = 3
STEPS = 64
LOCAL = 512
TILE = 16
TOKEN = TILE + NBAND * LOCAL
AXES = ("tm", "rows")


def route(up, down):
    pairs = []
    for step in range(STEPS):
        for half in range(2):
            for core, source in enumerate((up, down)):
                found = source(step, half)
                if found is None:
                    continue
                from_step, from_half = found
                pairs.append(
                    ((from_step % STEPS) * 4 + from_half * 2 + core, step * 4 + half * 2 + core)
                )
    return pairs


def above(t, h):
    return t + 1, h if t % 4 < 3 else 1 - h


def below(t, h):
    return (t - 1, h if t % 4 > 0 else 1 - h) if t > 0 else None


HOPS = (
    route(
        lambda t, h: (t - 4, h) if t % 4 == 3 else (t, h),
        lambda t, h: (t - 3, h if t % 4 < 3 else 1 - h),
    ),
    route(lambda t, h: (t - 1, h) if t % 4 > 0 else (t + 3, 1 - h), above),
    route(lambda t, h: (t - 1, h if t % 4 > 0 else 1 - h), above),
    route(below, lambda t, h: (t, h)),
)
SIBLING = [(i, i ^ 1) for i in range(STEPS * 4)]


def prepare_kernel(*refs):
    sources, token_ref, held, sems = refs[:5], refs[5], refs[6:11], refs[11]
    copies = [
        pltpu.make_async_copy(source, target, sems.at[n])
        for n, (source, target) in enumerate(zip(sources, held))
    ]
    for copy in copies:
        copy.start()
    for copy in copies:
        copy.wait()
    offsets_ref, band_ref, mask_ref, observed_ref, gain_ref = held
    flag = mask_ref[...].astype(jnp.float32)
    gain = gain_ref[...]
    factor = 1.0 - gain * flag
    vector = gain * flag * observed_ref[...]
    row = lax.broadcasted_iota(jnp.int32, (TILE, BLK), 0)
    lane = lax.broadcasted_iota(jnp.int32, (TILE, BLK), 1)
    tile = jnp.where(row == 0, jnp.broadcast_to(vector[:, :BLK], (TILE, BLK)), 0.0)
    tile = jnp.where(row == 1, jnp.broadcast_to(vector[:, BLK:], (TILE, BLK)), tile)
    for j in range(NBAND):
        shift = offsets_ref[0, j].astype(jnp.float32)
        tile = jnp.where((row == 2) & (lane == j), shift, tile)
    token_ref[:TILE, :] = tile.astype(jnp.bfloat16)
    for i in range(LOCAL // 128):
        column = jnp.transpose(
            jnp.broadcast_to(factor[:, i * 128 : (i + 1) * 128], (128, 128))
        )
        for j in range(NBAND):
            for side in range(2):
                lanes = slice(side * 128, side * 128 + 128)
                block = band_ref[0, j, i * 128 : (i + 1) * 128, lanes].astype(jnp.float32)
                top = TILE + j * LOCAL + i * 128
                token_ref[top : top + 128, lanes] = (column * block).astype(jnp.bfloat16)


def prepare(band, mask, observed, offsets, gain):
    return pl.pallas_call(
        prepare_kernel,
        out_shape=jax.ShapeDtypeStruct((TOKEN, BLK), jnp.bfloat16),
        in_specs=[pl.BlockSpec(memory_space=pltpu.HBM)] * 5,
        out_specs=pl.BlockSpec(memory_space=pltpu.VMEM),
        scratch_shapes=[
            pltpu.SMEM((1, NBAND), jnp.int32),
            pltpu.VMEM((1, NBAND, LOCAL, BLK), jnp.bfloat16),
            pltpu.VMEM((1, LOCAL), jnp.int32),
            pltpu.VMEM((1, LOCAL), jnp.float32),
            pltpu.VMEM((1, LOCAL), jnp.float32),
            pltpu.SemaphoreType.DMA((5,)),
        ],
    )(offsets, band, mask, observed, gain.reshape(1, LOCAL))


def tile_of(ref):
    return ref[:TILE, :].astype(jnp.float32)


def shifts_of(tile):
    row = lax.broadcasted_iota(jnp.int32, (TILE, BLK), 0)
    lane = lax.broadcasted_iota(jnp.int32, (TILE, BLK), 1)
    return [
        jnp.sum(jnp.where((row == 2) & (lane == j), tile, 0.0)).astype(jnp.int32)
        for j in range(NBAND)
    ]


def gather(refs, whole, distance, sems):
    step, place = lax.axis_index("tm"), lax.axis_index("rows")
    half = place // 2
    side = jnp.where(step % 4 >= distance, half, 1 - half)
    groups = [2 * side, 2 * side + 1, 2 * (1 - side) + 1, 2 * (1 - side)]
    rows = whole.shape[1]
    pairs = [
        [
            pltpu.make_async_copy(refs[4 * core + n].at[0:rows], whole.at[groups[n]], sems.at[n])
            for n in range(4)
        ]
        for core in range(2)
    ]

    def start():
        for core in range(2):

            @pl.when(place % 2 == core)
            def _():
                for copy in pairs[core]:
                    copy.start()

    def wait():
        for copy in pairs[0]:
            copy.wait()

    return start, wait


def column_of(source, earlier, shifts, c):
    product = None
    for j in range(NBAND):
        k = lax.rem(c - shifts[j] + NBLK, NBLK)
        at = pl.multiple_of(TILE + (2 * j + k % 2) * BLK, TILE)
        term = jnp.dot(
            source[k], earlier[k // 2, pl.ds(at, BLK), :], preferred_element_type=jnp.float32
        )
        product = term if product is None else product + term
    return product


def vector_of(tiles, c):
    return tiles[c // 2][c % 2 : c % 2 + 1, :]


def mark_kernel(value_ref, mark_ref):
    mark_ref[...] = jnp.zeros_like(mark_ref)


def mark(value):
    return pl.pallas_call(
        mark_kernel,
        out_shape=jax.ShapeDtypeStruct((8, 128), jnp.float32),
        in_specs=[pl.BlockSpec(memory_space=pl.ANY)],
        out_specs=pl.BlockSpec(memory_space=pltpu.VMEM),
        compiler_params=pltpu.CompilerParams(vmem_limit_bytes=1024 * 1024),
        cost_estimate=pl.CostEstimate(flops=0, bytes_accessed=4 * 2**20, transcendentals=0),
    )(value)


def place_kernel(own_ref, bare_ref, vector_ref):
    place = lax.axis_index("rows")
    tile = tile_of(own_ref)
    shifts = shifts_of(tile)
    bare_ref[...] = jnp.zeros_like(bare_ref)
    for j in range(NBAND):
        for r in range(2):
            target = lax.rem(2 * place + r + shifts[j] + NBLK, NBLK)
            at = TILE + (2 * j + r) * BLK
            bare_ref[target, r * BLK : (r + 1) * BLK, :] = own_ref[at : at + BLK, :]
    for r in range(2):
        vector_ref[:, r * BLK : (r + 1) * BLK] = tile[r : r + 1, :]


def place_blocks(own):
    vmem = pl.BlockSpec(memory_space=pltpu.VMEM)
    return pl.pallas_call(
        place_kernel,
        out_shape=[
            jax.ShapeDtypeStruct((NBLK, LOCAL, BLK), jnp.bfloat16),
            jax.ShapeDtypeStruct((1, LOCAL), jnp.float32),
        ],
        in_specs=[vmem],
        out_specs=[vmem, vmem],
        compiler_params=pltpu.CompilerParams(vmem_limit_bytes=8 * 1018 * 1024),
        cost_estimate=pl.CostEstimate(flops=1, bytes_accessed=1, transcendentals=0),
    )(own)


def weigh(matrix, tiles, start):
    parts = []
    for top in range(0, LOCAL, 64):
        rows = slice(top, top + 64)
        value = None if start is None else start[rows, :]
        for c in range(NBLK):
            term = matrix[c, rows, :].astype(jnp.float32) * vector_of(tiles, c)
            term = term[:, :128] + term[:, 128:]
            value = term if value is None else value + term
        parts.append(value)
    return jnp.concatenate(parts, axis=0)


def multiply(source, earlier, shifts, target):
    for c in range(NBLK):
        target[c] = column_of(source, earlier, shifts, c).astype(jnp.bfloat16)


def pair_kernel(*refs):
    bare, first, second, third = refs[0], refs[1:9], refs[9:17], refs[17:19]
    product_ref, total_ref, tile = refs[19:22]
    near, far, level, near_sems, far_sems, tile_sem = refs[22:]
    step = lax.axis_index("tm")
    near_start, near_wait = gather(first, near, 1, near_sems)
    far_start, far_wait = gather(second, far, 2, far_sems)
    tile_copies = [pltpu.make_async_copy(ref.at[0:TILE], tile, tile_sem.at[0]) for ref in third]
    for core in range(2):

        @pl.when(lax.axis_index("rows") % 2 == core)
        def _():
            tile_copies[core].start()

    near_start()
    far_start()
    tile_copies[0].wait()
    near_wait()
    far_wait()
    near_tiles = [tile_of(near.at[g]) for g in range(4)]
    far_tiles = [tile_of(far.at[g]) for g in range(4)]
    near_shifts, far_shifts = shifts_of(near_tiles[0]), shifts_of(far_tiles[0])

    @pl.when(step >= 2)
    def _():
        multiply(bare, near, near_shifts, level)
        total = weigh(bare, near_tiles, None)
        multiply(level, far, far_shifts, product_ref)
        total_ref[...] = weigh(level, far_tiles, total)

    @pl.when(step == 1)
    def _():
        multiply(bare, near, near_shifts, product_ref)
        total_ref[...] = weigh(bare, near_tiles, None)

    @pl.when(step == 0)
    def _():
        product_ref[...] = bare[...]
        total_ref[...] = jnp.zeros_like(total_ref)


def pair(bare, first, second, third):
    anywhere, vmem = pl.BlockSpec(memory_space=pl.ANY), pl.BlockSpec(memory_space=pltpu.VMEM)
    return pl.pallas_call(
        pair_kernel,
        out_shape=[
            jax.ShapeDtypeStruct((NBLK, LOCAL, BLK), jnp.bfloat16),
            jax.ShapeDtypeStruct((LOCAL, 128), jnp.float32),
            jax.ShapeDtypeStruct((TILE, BLK), jnp.bfloat16),
        ],
        in_specs=[vmem] + [anywhere] * 18,
        out_specs=[vmem, vmem, vmem],
        scratch_shapes=[
            pltpu.VMEM((4, TOKEN, BLK), jnp.bfloat16),
            pltpu.VMEM((4, TOKEN, BLK), jnp.bfloat16),
            pltpu.VMEM((NBLK, LOCAL, BLK), jnp.bfloat16),
            pltpu.SemaphoreType.DMA((4,)),
            pltpu.SemaphoreType.DMA((4,)),
            pltpu.SemaphoreType.DMA((1,)),
        ],
        compiler_params=pltpu.CompilerParams(vmem_limit_bytes=18 * 1024 * 1024),
        cost_estimate=pl.CostEstimate(flops=1, bytes_accessed=1, transcendentals=0),
    )(bare, *first, *second, *third)


def most_kernel(*refs):
    before, total_ref, tile, third = refs[0], refs[1], refs[2], refs[3:9]
    sum_ref, sum_total_ref = refs[9:11]
    earlier, sems = refs[11:]
    step, place = lax.axis_index("tm"), lax.axis_index("rows")
    side = jnp.where(step % 4 >= 3, place // 2, 1 - place // 2)
    groups = [2 * side, 2 * (1 - side) + 1, 2 * (1 - side)]
    pairs = [
        [
            pltpu.make_async_copy(third[3 * core + n], earlier.at[groups[n]], sems.at[n])
            for n in range(3)
        ]
        for core in range(2)
    ]
    for core in range(2):

        @pl.when(place % 2 == core)
        def _():
            for copy in pairs[core]:
                copy.start()

    earlier[2 * side + 1] = jnp.zeros((TOKEN, BLK), jnp.bfloat16)
    shifts = shifts_of(tile_of(tile))
    for copy in pairs[0]:
        copy.wait()

    @pl.when(step >= 3)
    def _():
        tiles = [tile_of(earlier.at[g]) for g in range(4)]
        sum_total_ref[...] = total_ref[...]
        for c in range(NBLK):
            sum_ref[c] = column_of(before, earlier, shifts, c)
            term = before[c].astype(jnp.float32) * vector_of(tiles, c)
            sum_total_ref[...] += term[:, :128] + term[:, 128:]

    @pl.when(step < 3)
    def _():
        sum_total_ref[...] = total_ref[...]
        for c in range(NBLK):
            sum_ref[c] = before[c].astype(jnp.float32)


def most(before, total, tile, third):
    anywhere, vmem = pl.BlockSpec(memory_space=pl.ANY), pl.BlockSpec(memory_space=pltpu.VMEM)
    return pl.pallas_call(
        most_kernel,
        out_shape=[
            jax.ShapeDtypeStruct((NBLK, LOCAL, BLK), jnp.float32),
            jax.ShapeDtypeStruct((LOCAL, 128), jnp.float32),
        ],
        in_specs=[vmem] * 3 + [anywhere] * 6,
        out_specs=[vmem, vmem],
        scratch_shapes=[
            pltpu.VMEM((4, TOKEN, BLK), jnp.bfloat16),
            pltpu.SemaphoreType.DMA((3,)),
        ],
        compiler_params=pltpu.CompilerParams(vmem_limit_bytes=14 * 1024 * 1024),
        cost_estimate=pl.CostEstimate(
            flops=48 * 2 * BLK**3, bytes_accessed=7 * 2**20, transcendentals=0
        ),
    )(before, total, tile, *third)


def last_kernel(*refs):
    before, sum_ref, total_ref, own_ref, tile, final = *refs[:5], refs[5:7]
    matrix_ref, vector_ref = refs[8:10]
    result, vector, out_sems = refs[10:]
    step, place = lax.axis_index("tm"), lax.axis_index("rows")
    group = 2 * jnp.where(step % 4 >= 3, place // 2, 1 - place // 2) + 1
    shifts = shifts_of(tile_of(tile))
    for core, piece in enumerate(final):

        @pl.when((step >= 3) & (place % 2 == core))
        def _():
            own_tile = tile_of(piece)
            total = total_ref[...]
            for r in range(2):
                k = 2 * group + r
                for j in range(NBAND):
                    at = TILE + (2 * j + r) * BLK
                    sum_ref[lax.rem(k + shifts[j] + NBLK, NBLK)] += jnp.dot(
                        before[k], piece[at : at + BLK, :], preferred_element_type=jnp.float32
                    )
                term = before[k].astype(jnp.float32) * own_tile[r : r + 1, :]
                total = total + (term[:, :128] + term[:, 128:])
            total_ref[...] = total

    writes = [
        pltpu.make_async_copy(
            result.at[c], matrix_ref.at[0, :, c * BLK : (c + 1) * BLK], out_sems.at[c]
        )
        for c in range(NBLK)
    ]
    writes.append(pltpu.make_async_copy(vector, vector_ref, out_sems.at[NBLK]))
    for c in range(NBLK):
        result[c] = sum_ref[c].astype(jnp.bfloat16)
        writes[c].start()
    total = total_ref[...]
    high = total.astype(jnp.bfloat16)
    low = (total - high.astype(jnp.float32)).astype(jnp.bfloat16)
    ones = jnp.ones((TILE, 128), jnp.bfloat16)
    sums = sum(
        lax.dot_general(ones, part, (((1,), (1,)), ((), ())), preferred_element_type=jnp.float32)
        for part in (high, low)
    )
    vector[...] = (sums[0:1, :] + own_ref[...]).astype(jnp.bfloat16)
    writes[NBLK].start()
    for write in writes:
        write.wait()


def last(before, partial, total, own, tile, final, mark):
    anywhere, vmem = pl.BlockSpec(memory_space=pl.ANY), pl.BlockSpec(memory_space=pltpu.VMEM)
    return pl.pallas_call(
        last_kernel,
        out_shape=[
            jax.ShapeDtypeStruct((1, LOCAL, NBLK * BLK), jnp.bfloat16),
            jax.ShapeDtypeStruct((1, LOCAL), jnp.bfloat16),
        ],
        in_specs=[vmem] * 7 + [anywhere],
        out_specs=[anywhere, anywhere],
        scratch_shapes=[
            pltpu.VMEM((NBLK, LOCAL, BLK), jnp.bfloat16),
            pltpu.VMEM((1, LOCAL), jnp.bfloat16),
            pltpu.SemaphoreType.DMA((NBLK + 1,)),
        ],
        compiler_params=pltpu.CompilerParams(vmem_limit_bytes=14 * 1024 * 1024),
        cost_estimate=pl.CostEstimate(
            flops=12 * 2 * BLK**3, bytes_accessed=7 * 2**20, transcendentals=0
        ),
    )(before, partial, total, own, tile, *final, mark)


def after(arrays, later, earlier):
    names = list(later) + list(earlier)
    tied = lax.optimization_barrier(tuple(arrays[n] for n in names))
    arrays.update(zip(names, tied))


def per_device(band_blocks, site_mask, observed, band_offsets, site_gain):
    x = {}

    def move(name, source, hop):
        x[name] = lax.ppermute(x[source], AXES, hop)

    x["0a"] = prepare(band_blocks, site_mask, observed, band_offsets, site_gain)
    move("0b", "0a", SIBLING)
    move("1a", "0a", HOPS[0])
    move("1b", "0b", HOPS[0])
    after(x, ["1a"], ["0b"])
    for n in (1, 2):
        for part in "ab":
            move(f"{n + 1}{part}", f"{n}{part}", HOPS[n])
    after(x, ["0a"], ["1b"])
    x["bare"], x["vector"] = place_blocks(x["0a"])
    move("s2a", "2a", SIBLING)
    move("s2b", "2b", SIBLING)
    after(x, ["3a"], ["bare", "s2a"])
    move("4a", "3a", HOPS[3])
    after(x, ["3b"], ["s2b"])
    move("s3a", "3a", SIBLING)
    move("s3b", "3b", SIBLING)
    move("4b", "3b", HOPS[3])
    after(x, ["1a", "1b"], ["2a"])
    move("s1a", "1a", SIBLING)
    move("s1b", "1b", SIBLING)
    after(x, ["bare"], ["4a"])
    x["product"], x["total"], tile = pair(
        x["bare"],
        [x[n] for n in ("2a", "2b", "s3a", "s3b", "s2a", "s2b", "3a", "3b")],
        [x[n] for n in ("3a", "3b", "s2a", "s2b", "s3a", "s3b", "2a", "2b")],
        [x["4a"], x["1a"]],
    )
    x["mark"] = mark(x["4a"])
    after(x, ["4a"], ["mark"])
    move("s4a", "4a", SIBLING)
    after(x, ["4b"], ["product", "s4a"])
    move("s4b", "4b", SIBLING)
    x["sum"], x["sum_total"] = most(
        x["product"],
        x["total"],
        tile,
        [x[n] for n in ("4a", "s1a", "s1b", "s4a", "1a", "1b")],
    )
    final = [x["4b"], x["s4b"]]
    return tuple(
        last(x["product"], x["sum"], x["sum_total"], x["vector"], tile, final, x["mark"])
    )


def solution(mesh):
    in_specs = (
        P("tm", None, "rows", None),
        P("tm", "rows"),
        P("tm", "rows"),
        P("tm", None),
        P("rows"),
    )
    out_specs = (P("tm", "rows", None), P("tm", "rows"))
    return jax.shard_map(
        per_device, mesh=mesh, in_specs=in_specs, out_specs=out_specs, check_vma=False
    )
```
